32 devices in a mesh: seq: 8 (over z, y), tp: 4 (over x, core).
Axes of the slice: x: 2, y: 2, z: 4, core: 2. Of those that a mesh axis runs over, the one named last changes fastest.
Arguments:
- tokens: bfloat16 [3072, 1024], P(('seq', 'tp')), may hold values from -6 to 6
- w_in: bfloat16 [3, 1024, 1024], P(None, None, 'tp'), may hold values from -0.1875 to 0.1875
- short_taps: float32 [3, 3, 1024], P(None, None, 'tp'), may hold values from -3.5 to 3.5
- skip_bias: float32 [2, 1024], P(None, 'tp'), may hold values from -4 to 4
- filter_spectra: float32 [2, 2, 16, 384, 1024], P(None, None, 'seq', None, 'tp'), may hold values from -6 to 6
- w_out: bfloat16 [1024, 1024], P('tp'), may hold values from -0.1875 to 0.1875
Outputs:
- mixed_out: bfloat16 [3072, 1024], P(('seq', 'tp'))
The draws below stay inside these ranges and needn't reach their ends.
All inputs are finite; a program needn't handle non-finite values.
Results may differ from the reference program's by a relative error of at most 0.007.
Values may be sent and summed in bfloat16 or wider, within the bound.
No kernel may reach another device: no remote copies, remote signals or barrier semaphores. Data moves between devices by JAX's collectives and lax.ppermute only.
A program may use at most 64 MiB of HBM per device.

```python
import math
import jax
import jax.numpy as jnp
from jax import lax

D = 1024
ROWS_DEV = 384
SEQ_LEN = 3072
FREQ_BLOCKS = 16


def shard_levels(key, dims, cuts, low, largest):
    def one(axis_at, parts):
        heights = jax.random.uniform(jax.random.fold_in(jax.random.fold_in(key, 6), axis_at), (parts,), jnp.float32, low / len(cuts), largest / len(cuts))
        return jnp.repeat(jnp.exp(heights), dims[axis_at] // parts).reshape((-1,) + (1,) * (len(dims) - axis_at - 1))

    gain = one(*cuts[0])
    for cut in cuts[1:]:
        gain = gain * one(*cut)
    return gain


def bell_draw(key, shape, scale, most, split=(), kind=jnp.bfloat16):
    drawn = scale * jax.random.normal(key, shape, jnp.float32)
    if split:
        drawn = drawn * shard_levels(key, shape, split, -0.22, 0.18)
    return jnp.clip(drawn, -most, most).astype(kind)


def setup_inputs(seed: int = 0) -> dict:
    keys = jax.random.split(jax.random.key(seed), 7)
    return {
        "tokens": bell_draw(keys[0], (SEQ_LEN, D), 1.0, 6.0, ((0, 32),)),
        "w_in": bell_draw(keys[1], (3, D, D), D ** -0.5, 0.1875, ((2, 4),)),
        "short_taps": bell_draw(keys[2], (3, 3, D), 3 ** -0.5, 3.5, ((2, 4),), jnp.float32),
        "skip_bias": bell_draw(keys[3], (2, D), 1.0, 4.0, ((1, 4),), jnp.float32),
        "filter_spectra": bell_draw(keys[4], (2, 2, FREQ_BLOCKS, ROWS_DEV, D), 1.0, 6.0, ((2, 8), (4, 4)), jnp.float32),
        "w_out": bell_draw(keys[5], (D, D), D ** -0.5, 0.1875, ((0, 4),)),
    }


def reference(tokens, w_in, short_taps, skip_bias, filter_spectra, w_out):
    length, features = tokens.shape
    blocks = filter_spectra.shape[2]
    positions = filter_spectra.shape[3]
    padded_len = blocks * positions
    block_width = math.gcd(features, 128)

    def one_block(block_id):
        offset = block_id * block_width
        weights = lax.dynamic_slice_in_dim(w_in, offset, block_width, 2)
        tap_block = lax.dynamic_slice_in_dim(short_taps, offset, block_width, 2)
        bias_block = lax.dynamic_slice_in_dim(skip_bias, offset, block_width, 1)
        spectra = lax.dynamic_slice_in_dim(filter_spectra, offset, block_width, 4)
        rounded = jnp.stack([jnp.dot(tokens, weights[branch_id], preferred_element_type=jnp.float32) for branch_id in range(3)]).astype(jnp.bfloat16)
        projected = lax.optimization_barrier(rounded).astype(jnp.float32)
        padded = jnp.pad(projected, ((0, 0), (2, 0), (0, 0)))
        filtered = tap_block[:, 0, None, :] * projected + tap_block[:, 1, None, :] * padded[:, 1:-1] + tap_block[:, 2, None, :] * padded[:, :-2]
        natural = jnp.swapaxes(spectra, 2, 3).reshape(2, 2, padded_len, block_width)
        carried = filtered[0]
        for order_index in range(2):
            spectrum = jnp.fft.fft(carried, n=padded_len, axis=0)
            response = lax.complex(natural[order_index, 0], natural[order_index, 1])
            convolved = jnp.real(jnp.fft.ifft(spectrum * response, axis=0))[:length]
            carried = filtered[order_index + 1] * (convolved + bias_block[order_index] * carried)
        return carried.astype(jnp.bfloat16)

    pieces = lax.map(one_block, jnp.arange(features // block_width, dtype=jnp.int32))
    hidden = jnp.moveaxis(pieces, 0, 1).reshape(length, features)
    return jnp.dot(hidden, w_out, preferred_element_type=jnp.float32).astype(jnp.bfloat16)
```

```python
import functools
import math

import jax
import jax.numpy as jnp
import numpy as np
from jax import lax
from jax.experimental import pallas as pl
from jax.experimental.pallas import tpu as pltpu
from jax.sharding import PartitionSpec as P

VMEM = pl.BlockSpec(memory_space=pltpu.VMEM)
LIMIT = 48 * 1024 * 1024


def line_table(length):
    phases = np.outer(np.arange(length), np.arange(length)) % length
    angles = 2.0 * np.pi / length * phases
    cos, sin = np.cos(angles), np.sin(angles)
    return jnp.asarray(np.block([[cos, -sin], [sin, cos]]), jnp.bfloat16)


def twist_tables(blocks, length):
    angles = 2.0 * np.pi / (blocks * length) * np.outer(np.arange(blocks), np.arange(length))
    cos, sin = np.cos(angles), np.sin(angles)
    return jnp.asarray(np.stack([cos, -sin]), jnp.float32)


def plus(a, b):
    return b if a is None else a if b is None else a + b


def minus(a, b):
    return a if b is None else -b if a is None else a - b


def times(pair, k, size, direction):
    re, im = pair
    cos, sin = math.cos(2 * math.pi * k / size), direction * math.sin(2 * math.pi * k / size)
    return re * cos - im * sin, re * sin + im * cos


def forward_half(values):
    if len(values) == 1:
        return [(values[0], None), (values[0], None)]
    even, odd = forward_half(values[0::2]), forward_half(values[1::2])
    half = len(values)
    quarter = half // 2
    out = [None] * (half + 1)
    out[0] = (even[0][0] + odd[0][0], None)
    out[half] = (even[0][0] - odd[0][0], None)
    out[quarter] = (even[quarter][0], -odd[quarter][0])
    for k in range(1, quarter):
        re, im = times(odd[k], k, 2 * half, -1.0)
        out[k] = (even[k][0] + re, even[k][1] + im)
        out[half - k] = (even[k][0] - re, im - even[k][1])
    return out


def inverse_half(bins):
    half = len(bins) - 1
    if half == 1:
        return [bins[0][0] + bins[1][0]]
    quarter = half // 2
    even = [(bins[0][0] + bins[half][0], None)]
    odd = [(bins[0][0] - bins[half][0], None)]
    for k in range(1, quarter):
        (a, b), (c, d) = bins[k], bins[half - k]
        even.append((a + c, b - d))
        odd.append(times((a - c, b + d), k, 2 * half, 1.0))
    even.append((2.0 * bins[quarter][0], None))
    odd.append((-2.0 * bins[quarter][1], None))
    out = [None] * half
    out[0::2] = inverse_half(even)
    out[1::2] = inverse_half(odd)
    return out


def spectra_kernel(spectra_ref, out_ref):
    turned = spectra_ref[0, 0, 0].T
    shape = out_ref.shape
    out_ref[:, 0] = turned.reshape(shape[0], shape[2], shape[3]).astype(jnp.bfloat16)


def send_spectra(spectra, count):
    orders, parts, residues, length, channels = spectra.shape
    each = channels // count
    slabs = orders * parts * residues
    return pl.pallas_call(
        spectra_kernel,
        grid=(slabs,),
        in_specs=[
            pl.BlockSpec(
                (1, 1, 1, length, channels),
                lambda i: (i // (parts * residues), i // residues % parts, i % residues, 0, 0),
            )
        ],
        out_specs=pl.BlockSpec((count, 1, each, length), lambda i: (0, i, 0, 0)),
        out_shape=jax.ShapeDtypeStruct((count, slabs, each, length), jnp.bfloat16),
        compiler_params=pltpu.CompilerParams(vmem_limit_bytes=LIMIT),
    )(spectra)


def project_kernel(tokens_ref, weight_ref, *refs):
    outs, held = refs[:-1], refs[-1]
    count, pieces, each, length = held.shape
    me = lax.axis_index("seq")
    rows = jnp.dot(tokens_ref[...], weight_ref[0], preferred_element_type=jnp.float32)
    for piece in range(pieces):
        turned = rows[piece * length : (piece + 1) * length].T
        held[:, piece] = turned.reshape(count, each, length).astype(jnp.bfloat16)
    for shift, out in enumerate(outs):
        out[0] = held[lax.rem(me + shift, count)]


def project(tokens, weights, count, length):
    rows, depth = tokens.shape
    branches, _, channels = weights.shape
    each, pieces = channels // count, rows // length
    return pl.pallas_call(
        project_kernel,
        grid=(branches,),
        in_specs=[
            pl.BlockSpec((rows, depth), lambda b: (0, 0)),
            pl.BlockSpec((1, depth, channels), lambda b: (b, 0, 0)),
        ],
        out_specs=[pl.BlockSpec((1, pieces, each, length), lambda b: (b, 0, 0, 0))] * count,
        out_shape=[jax.ShapeDtypeStruct((branches, pieces, each, length), jnp.bfloat16)] * count,
        scratch_shapes=[pltpu.VMEM((count, pieces, each, length), jnp.bfloat16)],
        compiler_params=pltpu.CompilerParams(vmem_limit_bytes=LIMIT),
    )(tokens, weights)


def convolve_kernel(count, *refs):
    arrived, refs = refs[:count], refs[count:]
    spectra_ref, taps_ref, skip_ref, table_ref, twist_ref, out_ref = refs[:6]
    held, filtered, lines, wave, gathered, columns = refs[6:]
    branches, positions, each, length = filtered.shape
    residues = spectra_ref.shape[1] // 4
    blocks = count * residues
    pieces = positions // count
    me = lax.axis_index("seq")
    chunk = min(16, each)
    width = 128

    for shift in range(count):
        held[lax.rem(me - shift + count, count)] = arrived[shift][...]

    for branch in range(branches):
        gathered[branch * 3 : branch * 3 + 3] = taps_ref[branch]
    gathered[9:11] = skip_ref[...]
    columns[...] = gathered[...].T
    mine = columns[pl.ds(pl.multiple_of(me * each, each), each), :]
    lane = lax.broadcasted_iota(jnp.int32, (each, length), 1)
    for branch in range(branches):
        last = [jnp.zeros((each, length), jnp.float32)] * 2
        scale = [jnp.broadcast_to(mine[:, branch * 3 + i : branch * 3 + i + 1], (each, length)) for i in range(3)]
        for p in range(positions):
            now = held[p // pieces, branch, p % pieces].astype(jnp.float32)
            total = scale[0] * now
            for back in (1, 2):
                rolled = pltpu.roll(now, back, 1)
                total = total + scale[back] * jnp.where(lane < back, last[back - 1], rolled)
                last[back - 1] = rolled
            filtered[branch, p] = total

    tiles = [(r, c) for r in range(0, each, chunk) for c in range(0, length, width)]
    step = max(each, min(blocks * each, 128))
    for order in range(2):
        for r, c in tiles:
            bins = forward_half([filtered[0, p, r : r + chunk, c : c + width] for p in range(positions)])
            for k in range(blocks):
                cos, sin = twist_ref[0, k : k + 1, c : c + width], twist_ref[1, k : k + 1, c : c + width]
                re, im = bins[min(k, blocks - k)]
                if im is None:
                    pair = (re * cos, re * sin)
                elif 2 * k < blocks:
                    pair = (re * cos - im * sin, re * sin + im * cos)
                else:
                    pair = (re * cos + im * sin, re * sin - im * cos)
                for part in range(2):
                    lines[k * each + r : k * each + r + chunk, part * length + c : part * length + c + width] = pair[part].astype(jnp.bfloat16)
        for start in range(0, blocks * each, step):
            spectrum = jnp.dot(lines[start : start + step], table_ref[...], preferred_element_type=jnp.float32)
            for k in range(start // each, (start + step) // each):
                at = k * each - start
                re, im = spectrum[at : at + each, :length], spectrum[at : at + each, length:]
                first = order * 2 * residues + k % residues
                gain_re = spectra_ref[k // residues, first].astype(jnp.float32)
                gain_im = spectra_ref[k // residues, first + residues].astype(jnp.float32)
                lines[k * each : (k + 1) * each, :length] = (re * gain_re - im * gain_im).astype(jnp.bfloat16)
                lines[k * each : (k + 1) * each, length:] = (-(re * gain_im) - im * gain_re).astype(jnp.bfloat16)
        for start in range(0, blocks * each, step):
            wave[start : start + step] = jnp.dot(lines[start : start + step], table_ref[...], preferred_element_type=jnp.float32)
        for r, c in tiles:
            turned = []
            for k in range(blocks):
                cos, sin = twist_ref[0, k : k + 1, c : c + width], twist_ref[1, k : k + 1, c : c + width]
                re = wave[k * each + r : k * each + r + chunk, c : c + width]
                im = wave[k * each + r : k * each + r + chunk, length + c : length + c + width]
                turned.append((re * cos - im * sin, re * sin + im * cos))
            bins = [(turned[0][0] * 2.0, None)]
            for k in range(1, blocks // 2):
                one, two = turned[k], turned[blocks - k]
                bins.append((one[0] + two[0], two[1] - one[1]))
            bins.append((turned[blocks // 2][0] * 2.0, None))
            values = inverse_half(bins)
            skip = columns[pl.ds(pl.multiple_of(me * each + r, chunk), chunk), 9 + order : 10 + order]
            for p in range(positions):
                here = (p, slice(r, r + chunk), slice(c, c + width))
                carried = filtered[(0,) + here]
                total = values[p] * (0.5 / (blocks * length)) + skip * carried
                filtered[(0,) + here] = filtered[(order + 1,) + here] * total

    share, across = out_ref.shape[3], out_ref.shape[1]
    for p in range(positions):
        for part in range(length // share):
            to = p % pieces * (length // share) + part
            out_ref[p // pieces, to] = filtered[0, p, :, part * share : (part + 1) * share].astype(jnp.bfloat16)


def convolve(arrived, spectra, taps, skip, across):
    count, slabs, each, length = spectra.shape
    branches, pieces = arrived[0].shape[:2]
    blocks = count * (slabs // 4)
    positions = count * pieces
    channels = taps.shape[2]
    share = pieces * length // across
    return pl.pallas_call(
        functools.partial(convolve_kernel, count),
        in_specs=[VMEM] * (count + 5),
        out_specs=VMEM,
        out_shape=jax.ShapeDtypeStruct((count, across, each, share), jnp.bfloat16),
        scratch_shapes=[
            pltpu.VMEM((count, branches, pieces, each, length), jnp.bfloat16),
            pltpu.VMEM((branches, positions, each, length), jnp.float32),
            pltpu.VMEM((blocks * each, 2 * length), jnp.bfloat16),
            pltpu.VMEM((blocks * each, 2 * length), jnp.float32),
            pltpu.VMEM((16, channels), jnp.float32),
            pltpu.VMEM((channels, 16), jnp.float32),
        ],
        compiler_params=pltpu.CompilerParams(vmem_limit_bytes=LIMIT),
    )(*arrived, spectra, taps, skip, line_table(length), twist_tables(blocks, length))


def finish_kernel(gated_ref, *refs):
    weights, out_ref = refs[:-1], refs[-1]
    count, across, each, share = gated_ref.shape
    me = lax.axis_index("tp")
    total = jnp.zeros(out_ref.shape, jnp.float32)
    for flip, weight in enumerate(weights):
        part = gated_ref[:, jnp.bitwise_xor(me, flip)].astype(jnp.float32)
        part = part.reshape(count * each, share).astype(jnp.bfloat16)
        total = total + lax.dot_general(
            part, weight[...], (((0,), (0,)), ((), ())), preferred_element_type=jnp.float32
        )
    out_ref[...] = total.astype(jnp.bfloat16)


def finish(gated, weights):
    across, share, width = gated.shape[1], gated.shape[3], weights[0].shape[1]
    return pl.pallas_call(
        finish_kernel,
        in_specs=[VMEM] * (1 + across),
        out_specs=VMEM,
        out_shape=jax.ShapeDtypeStruct((share, width), jnp.bfloat16),
        compiler_params=pltpu.CompilerParams(vmem_limit_bytes=LIMIT),
    )(gated, *weights)


def local(tokens, w_in, short_taps, skip_bias, filter_spectra, w_out):
    count, across = lax.axis_size("seq"), lax.axis_size("tp")
    length = filter_spectra.shape[3]
    spectra = send_spectra(filter_spectra, count)
    spectra = lax.all_to_all(spectra, "seq", split_axis=0, concat_axis=0, tiled=True)
    gathered = lax.all_gather(tokens, "tp", axis=0, tiled=True)
    outgoing = project(gathered, w_in, count, length)
    arrived = [outgoing[0]] + [
        lax.ppermute(outgoing[shift], "seq", [(i, (i + shift) % count) for i in range(count)])
        for shift in range(1, count)
    ]
    weights = [w_out] + [
        lax.ppermute(w_out, "tp", [(i, i ^ flip) for i in range(across)]) for flip in range(1, across)
    ]
    gated = convolve(arrived, spectra, short_taps, skip_bias, across)
    shape = gated.shape
    gated = gated.reshape((count * across,) + shape[2:])
    gated = lax.all_to_all(gated, ("seq", "tp"), split_axis=0, concat_axis=0, tiled=True)
    return finish(gated.reshape(shape), weights)


def solution(mesh):
    in_specs = (
        P(("seq", "tp"), None),
        P(None, None, "tp"),
        P(None, None, "tp"),
        P(None, "tp"),
        P(None, None, "seq", None, "tp"),
        P("tp", None),
    )
    out_specs = P(("seq", "tp"), None)
    return jax.shard_map(local, mesh=mesh, in_specs=in_specs, out_specs=out_specs, check_vma=False)
```

```python
import functools
import math

import jax
import jax.numpy as jnp
import numpy as np
from jax import lax
from jax.experimental import pallas as pl
from jax.experimental.pallas import tpu as pltpu
from jax.sharding import PartitionSpec as P

VMEM = pl.BlockSpec(memory_space=pltpu.VMEM)
ANY = pl.BlockSpec(memory_space=pl.ANY)
MOST = 63 * 1024 * 1024
LANES = 128
INNER = 16
LIMIT = 20 * 1024 * 1024


def phase_rows(blocks, length):
    line = np.arange(length)
    angles = [
        2.0 * np.pi / (blocks * length) * np.outer(np.arange(blocks), line),
        2.0 * np.pi / length * (np.outer(INNER * np.arange(length // INNER), line) % length),
        2.0 * np.pi / length * (np.outer(np.arange(INNER), line) % length),
    ]
    return jnp.asarray(np.concatenate([part for a in angles for part in (np.cos(a), -np.sin(a))]), jnp.float32)


def build_table(phases_ref, top, table_ref):
    length = phases_ref.shape[1]
    outer = length // INNER
    cos_j, sin_j = phases_ref[top + 2 * outer : top + 2 * outer + INNER], phases_ref[top + 2 * outer + INNER :]
    for i in range(outer):
        cos_i, sin_i = phases_ref[top + i : top + i + 1], phases_ref[top + outer + i : top + outer + i + 1]
        cos = (cos_i * cos_j - sin_i * sin_j).astype(jnp.bfloat16)
        sin = (cos_i * sin_j + sin_i * cos_j).astype(jnp.bfloat16)
        table_ref[i * INNER : (i + 1) * INNER, :length] = cos
        table_ref[i * INNER : (i + 1) * INNER, length:] = sin
        table_ref[length + i * INNER : length + (i + 1) * INNER, :length] = -sin
        table_ref[length + i * INNER : length + (i + 1) * INNER, length:] = cos


def window_width(share, count):
    return -(-(share + 2 * count) // LANES) * LANES


def share_table(length, share, wide):
    columns = np.arange(length)
    table = np.zeros((length, length // share * wide))
    table[columns, columns // share * wide + columns % share] = 1.0
    return jnp.asarray(table, jnp.bfloat16)


def times(pair, k, size, direction):
    re, im = pair
    cos, sin = math.cos(2 * math.pi * k / size), direction * math.sin(2 * math.pi * k / size)
    return re * cos - im * sin, re * sin + im * cos


def forward_half(values):
    if len(values) == 1:
        return [(values[0], None), (values[0], None)]
    even, odd = forward_half(values[0::2]), forward_half(values[1::2])
    half = len(values)
    quarter = half // 2
    out = [None] * (half + 1)
    out[0] = (even[0][0] + odd[0][0], None)
    out[half] = (even[0][0] - odd[0][0], None)
    out[quarter] = (even[quarter][0], -odd[quarter][0])
    for k in range(1, quarter):
        re, im = times(odd[k], k, 2 * half, -1.0)
        out[k] = (even[k][0] + re, even[k][1] + im)
        out[half - k] = (even[k][0] - re, im - even[k][1])
    return out


def inverse_half(bins):
    half = len(bins) - 1
    if half == 1:
        return [bins[0][0] + bins[1][0]]
    quarter = half // 2
    even = [(bins[0][0] + bins[half][0], None)]
    odd = [(bins[0][0] - bins[half][0], None)]
    for k in range(1, quarter):
        (a, b), (c, d) = bins[k], bins[half - k]
        even.append((a + c, b - d))
        odd.append(times((a - c, b + d), k, 2 * half, 1.0))
    even.append((2.0 * bins[quarter][0], None))
    odd.append((-2.0 * bins[quarter][1], None))
    out = [None] * half
    out[0::2] = inverse_half(even)
    out[1::2] = inverse_half(odd)
    return out


def spectra_kernel(spectra_ref, out_ref, arriving, leaving, sems_in, sems_out):
    orders, parts, residues = spectra_ref.shape[:3]
    count, slabs, each, length = out_ref.shape
    fetches, stores = [], []
    for i in range(slabs):
        order, part, residue = i // (parts * residues), i // residues % parts, i % residues
        fetches.append(
            pltpu.make_async_copy(spectra_ref.at[order, part, residue], arriving.at[i], sems_in.at[i])
        )
        stores.append(pltpu.make_async_copy(leaving.at[i], out_ref.at[:, i], sems_out.at[i]))
    for fetch in fetches:
        fetch.start()
    for i, (fetch, store) in enumerate(zip(fetches, stores)):
        fetch.wait()
        leaving[i] = arriving[i].T.reshape(count, each, length).astype(jnp.bfloat16)
        store.start()
    for store in stores:
        store.wait()


def send_spectra(spectra, count):
    orders, parts, residues, length, channels = spectra.shape
    each = channels // count
    slabs = orders * parts * residues
    return pl.pallas_call(
        spectra_kernel,
        in_specs=[ANY],
        out_specs=ANY,
        out_shape=jax.ShapeDtypeStruct((count, slabs, each, length), jnp.bfloat16),
        scratch_shapes=[
            pltpu.VMEM((slabs, length, channels), jnp.float32),
            pltpu.VMEM((slabs, count, each, length), jnp.bfloat16),
            pltpu.SemaphoreType.DMA((slabs,)),
            pltpu.SemaphoreType.DMA((slabs,)),
        ],
        compiler_params=pltpu.CompilerParams(vmem_limit_bytes=MOST),
    )(spectra)


def tap_columns(taps_ref, skip_ref, gathered):
    branches = taps_ref.shape[0]
    for branch in range(branches):
        gathered[branch * 3 : branch * 3 + 3] = taps_ref[branch]
    gathered[9:11] = skip_ref[...]
    return gathered[...].T


def filter_lines(now, last, scale, lane):
    total = scale[0] * now
    rolls = []
    for back in (1, 2):
        rolled = pltpu.roll(now, back, 1)
        total = total + scale[back] * jnp.where(lane < back, last[back - 1], rolled)
        rolls.append(rolled)
    return total, rolls


def project_kernel(tokens_ref, weight_ref, taps_ref, skip_ref, *refs):
    mine_ref, other_ref, edge_ref = refs[:3]
    outs, (held, gathered, windows) = refs[3:-3], refs[-3:]
    count, pieces, each, length = held.shape
    across, channels, wide = windows.shape
    share = pieces * length // across
    branch = pl.program_id(0)
    me = lax.axis_index("seq")
    rows = jnp.dot(tokens_ref[...], weight_ref[0], preferred_element_type=jnp.float32)
    turned = [rows[piece * length : (piece + 1) * length].T for piece in range(pieces)]

    @pl.when(branch < 2)
    def _():
        for piece in range(pieces):
            held[:, piece] = turned[piece].reshape(count, each, length).astype(jnp.bfloat16)
        for shift in range(count // 2):
            to = lax.rem(me + 2 * shift, count)
            mine_ref[shift, 0] = held[to]
            other_ref[shift, 0] = held[jnp.bitwise_xor(to, 1)]

    @pl.when(branch == 2)
    def _():
        columns = tap_columns(taps_ref, skip_ref, gathered)
        scale = [jnp.broadcast_to(columns[:, 6 + i : 7 + i], (channels, length)) for i in range(3)]
        lane = lax.broadcasted_iota(jnp.int32, (channels, length), 1)
        last = [jnp.zeros((channels, length), jnp.float32)] * 2
        windows[...] = jnp.zeros_like(windows)
        for piece in range(pieces):
            now = turned[piece].astype(jnp.bfloat16).astype(jnp.float32)
            total, last = filter_lines(now, last, scale, lane)
            for part in range(length // share):
                window = total[:, part * share : (part + 1) * share]
                windows[piece * (length // share) + part, :, :share] = window.astype(jnp.bfloat16)
        for flip, out in enumerate(outs):
            out[...] = windows[jnp.bitwise_xor(lax.axis_index("tp"), flip)]
        edge = jnp.where(lane < 1, scale[1] * last[0], 0.0) + jnp.where(lane < 2, scale[2] * last[1], 0.0)
        edge = edge[:, :LANES] * (me < count - 1).astype(jnp.float32)
        if wide > LANES:
            edge = jnp.concatenate([edge, jnp.zeros((channels, wide - LANES), jnp.float32)], axis=1)
        total = jnp.zeros((each, wide), jnp.float32)
        for block in range(count):
            total = total + pltpu.roll(edge[block * each : (block + 1) * each], share + 2 * block, 1)
        edge_ref[...] = total.astype(jnp.bfloat16)


def project(tokens, weights, taps, skip, count, across, length):
    rows, depth = tokens.shape
    branches, _, channels = weights.shape
    each, pieces = channels // count, rows // length
    wide = window_width(rows // across, count)
    half = (count // 2, 1, pieces, each, length)
    return pl.pallas_call(
        project_kernel,
        grid=(branches,),
        in_specs=[
            pl.BlockSpec((rows, depth), lambda b: (0, 0)),
            pl.BlockSpec((1, depth, channels), lambda b: (b, 0, 0)),
            pl.BlockSpec(taps.shape, lambda b: (0, 0, 0)),
            pl.BlockSpec(skip.shape, lambda b: (0, 0)),
        ],
        out_specs=[
            pl.BlockSpec(half, lambda b: (0, jnp.minimum(b, 1), 0, 0, 0)),
            pl.BlockSpec(half, lambda b: (0, jnp.minimum(b, 1), 0, 0, 0)),
            pl.BlockSpec((each, wide), lambda b: (0, 0)),
        ]
        + [pl.BlockSpec((channels, wide), lambda b: (0, 0))] * across,
        out_shape=[
            jax.ShapeDtypeStruct((count // 2, 2) + half[2:], jnp.bfloat16),
            jax.ShapeDtypeStruct((count // 2, 2) + half[2:], jnp.bfloat16),
            jax.ShapeDtypeStruct((each, wide), jnp.bfloat16),
        ]
        + [jax.ShapeDtypeStruct((channels, wide), jnp.bfloat16)] * across,
        scratch_shapes=[
            pltpu.VMEM((count, pieces, each, length), jnp.bfloat16),
            pltpu.VMEM((16, channels), jnp.float32),
            pltpu.VMEM((across, channels, wide), jnp.bfloat16),
        ],
        compiler_params=pltpu.CompilerParams(vmem_limit_bytes=LIMIT),
    )(tokens, weights, taps, skip)


def pack_kernel(weight_ref, *refs):
    windows, outs = refs[: len(refs) // 2], refs[len(refs) // 2 :]
    for window, out in zip(windows, outs):
        wide = window.shape[1]
        out[:, :wide] = window[...]
        out[:, wide:] = weight_ref[...]


def pack(windows, weight):
    channels, wide = windows[0].shape
    shape = jax.ShapeDtypeStruct((channels, wide + weight.shape[1]), jnp.bfloat16)
    return pl.pallas_call(
        pack_kernel,
        in_specs=[VMEM] * (1 + len(windows)),
        out_specs=[VMEM] * len(windows),
        out_shape=[shape] * len(windows),
        compiler_params=pltpu.CompilerParams(vmem_limit_bytes=LIMIT),
    )(weight, *windows)


def relay_kernel(mine_ref, came_ref, *outs):
    for shift, out in enumerate(outs, 1):
        out[0] = mine_ref[shift]
        out[1] = came_ref[shift]


def relay(mine, came):
    shape = (2,) + mine.shape[1:]
    return pl.pallas_call(
        relay_kernel,
        in_specs=[VMEM] * 2,
        out_specs=[VMEM] * (mine.shape[0] - 1),
        out_shape=[jax.ShapeDtypeStruct(shape, jnp.bfloat16)] * (mine.shape[0] - 1),
        compiler_params=pltpu.CompilerParams(vmem_limit_bytes=LIMIT),
    )(mine, came)


def tiles_of(each, length):
    chunk, width = min(16, each), 128
    return [(slice(r, r + chunk), slice(c, c + width)) for r in range(0, each, chunk) for c in range(0, length, width)]


def part_of(cols, length, part):
    return slice(part * length + cols.start, part * length + cols.stop)


def twist_of(phases_ref, k, blocks, cols):
    return phases_ref[k : k + 1, cols], phases_ref[blocks + k : blocks + k + 1, cols]


def forward_tile(values, tile, lines, phases_ref, each, length):
    rows, cols = tile
    blocks = 2 * len(values)
    bins = forward_half(values)
    for k in range(blocks):
        cos, sin = twist_of(phases_ref, k, blocks, cols)
        re, im = bins[min(k, blocks - k)]
        if im is None:
            pair = (re * cos, re * sin)
        elif 2 * k < blocks:
            pair = (re * cos - im * sin, re * sin + im * cos)
        else:
            pair = (re * cos + im * sin, re * sin - im * cos)
        at = slice(k * each + rows.start, k * each + rows.stop)
        for part in range(2):
            lines[at, part_of(cols, length, part)] = pair[part].astype(jnp.bfloat16)


def respond(spectrum, start, order, spectra_ref, lines, each, length):
    residues = spectra_ref.shape[1] // 4
    for k in range(start // each, (start + spectrum.shape[0]) // each):
        at = k * each - start
        re, im = spectrum[at : at + each, :length], spectrum[at : at + each, length:]
        first = order * 2 * residues + k % residues
        gain_re = spectra_ref[k // residues, first].astype(jnp.float32)
        gain_im = spectra_ref[k // residues, first + residues].astype(jnp.float32)
        lines[k * each : (k + 1) * each, :length] = (re * gain_re - im * gain_im).astype(jnp.bfloat16)
        lines[k * each : (k + 1) * each, length:] = (-(re * gain_im) - im * gain_re).astype(jnp.bfloat16)


def inverse_tile(wave, tile, phases_ref, positions, each, length):
    rows, cols = tile
    blocks = 2 * positions
    turned = []
    for k in range(blocks):
        cos, sin = twist_of(phases_ref, k, blocks, cols)
        at = slice(k * each + rows.start, k * each + rows.stop)
        re, im = wave[at, cols], wave[at, part_of(cols, length, 1)]
        turned.append((re * cos - im * sin, re * sin + im * cos))
    bins = [(turned[0][0] * 2.0, None)]
    for k in range(1, positions):
        one, two = turned[k], turned[blocks - k]
        bins.append((one[0] + two[0], two[1] - one[1]))
    bins.append((turned[positions][0] * 2.0, None))
    return [value * (0.5 / (blocks * length)) for value in inverse_half(bins)]


def row_steps(blocks, each):
    step = max(each, min(blocks * each, 128))
    return [slice(start, start + step) for start in range(0, blocks * each, step)]


def flipped(array, flip, size):
    return lax.ppermute(array, "tp", [(i, i ^ flip) for i in range(size)])


def convolve_kernel(*refs):
    mine_in, came_in, spectra_in, phases_in, shares_in, taps_ref, skip_ref, edge_ref = refs[:8]
    shifted, refs = refs[8:-14], refs[-14:]
    out_ref, held, spectra_ref, phases_ref, shares_ref, table_ref, filtered, lines, wave = refs[:9]
    gathered, columns, leaving, sems, some = refs[9:]
    branches, positions, each, length = filtered.shape
    blocks = 2 * positions
    count = held.shape[0]
    pieces = positions // count
    slabs = spectra_ref.shape[1]
    me = lax.axis_index("seq")
    other = jnp.bitwise_xor(me, 1)

    inward = [
        pltpu.make_async_copy(mine_in.at[0], held.at[me], some.at[0]),
        pltpu.make_async_copy(came_in.at[0], held.at[other], some.at[1]),
    ]
    for shift, ref in enumerate(shifted, 1):
        for i, one in enumerate((me, other)):
            source = lax.rem(one + count - 2 * shift, count)
            inward.append(pltpu.make_async_copy(ref.at[i], held.at[source], some.at[2 * shift + i]))
    halves = [slice(0, slabs // 2), slice(slabs // 2, slabs)]
    phases = pltpu.make_async_copy(phases_in, phases_ref, sems.at[0])
    spectra = [
        pltpu.make_async_copy(spectra_in.at[:, half], spectra_ref.at[:, half], sems.at[1 + i])
        for i, half in enumerate(halves)
    ]
    shares = pltpu.make_async_copy(shares_in, shares_ref, sems.at[3])
    for copy in [phases] + inward:
        copy.start()
    columns[...] = tap_columns(taps_ref, skip_ref, gathered)
    mine = columns[pl.ds(pl.multiple_of(me * each, each), each), :]
    lane = lax.broadcasted_iota(jnp.int32, (each, length), 1)
    phases.wait()
    for copy in inward:
        copy.wait()
    for copy in spectra + [shares]:
        copy.start()
    build_table(phases_ref, 2 * blocks, table_ref)
    for branch in range(branches):
        last = [jnp.zeros((each, length), jnp.float32)] * 2
        scale = [jnp.broadcast_to(mine[:, branch * 3 + i : branch * 3 + i + 1], (each, length)) for i in range(3)]
        for p in range(positions):
            now = held[p // pieces, branch, p % pieces].astype(jnp.float32)
            filtered[branch, p], last = filter_lines(now, last, scale, lane)
    skips = [jnp.broadcast_to(mine[:, 9 + order : 10 + order], (each, LANES)) for order in range(2)]

    def through(order):
        spectra[order].wait()
        for rows in row_steps(blocks, each):
            spectrum = jnp.dot(lines[rows], table_ref[...], preferred_element_type=jnp.float32)
            respond(spectrum, rows.start, order, spectra_ref, lines, each, length)
        for rows in row_steps(blocks, each):
            wave[rows] = jnp.dot(lines[rows], table_ref[...], preferred_element_type=jnp.float32)

    tiles = tiles_of(each, length)
    for tile in tiles:
        forward_tile([filtered[(0, p) + tile] for p in range(positions)], tile, lines, phases_ref, each, length)
    through(0)
    for tile in tiles:
        values = inverse_tile(wave, tile, phases_ref, positions, each, length)
        for p, value in enumerate(values):
            values[p] = filtered[(1, p) + tile] * (value + skips[0][tile[0]] * filtered[(0, p) + tile])
            filtered[(0, p) + tile] = values[p]
        forward_tile(values, tile, lines, phases_ref, each, length)
    through(1)
    for tile in tiles:
        for p, value in enumerate(inverse_tile(wave, tile, phases_ref, positions, each, length)):
            filtered[(0, p) + tile] = value + skips[1][tile[0]] * filtered[(0, p) + tile]
    shares.wait()
    wide = out_ref.shape[3]
    parts = shares_ref.shape[1] // wide
    flat = filtered[0].reshape(positions * each, length).astype(jnp.bfloat16)
    spread_out = jnp.dot(flat, shares_ref[...], preferred_element_type=jnp.float32)
    for p in range(positions):
        for part in range(parts):
            block = spread_out[p * each : (p + 1) * each, part * wide : (part + 1) * wide]
            leaving[p // pieces, p % pieces * parts + part] = block.astype(jnp.bfloat16)
    following = lax.rem(me + 1, count)
    leaving[following, 0] = leaving[following, 0] + edge_ref[...]
    store = pltpu.make_async_copy(leaving, out_ref, sems.at[4])
    store.start()
    store.wait()


def convolve(mine, came, shifted, spectra, taps, skip, edge, across):
    count, slabs, each, length = spectra.shape
    branches, pieces = mine.shape[1:3]
    positions = count * pieces
    blocks = 2 * positions
    channels = taps.shape[2]
    phases = phase_rows(blocks, length)
    share = pieces * length // across
    wide = window_width(share, count)
    shares = share_table(length, share, wide)
    return pl.pallas_call(
        convolve_kernel,
        in_specs=[ANY] * 5 + [VMEM] * 3 + [ANY] * len(shifted),
        out_specs=ANY,
        out_shape=jax.ShapeDtypeStruct((count, across, each, wide), jnp.bfloat16),
        scratch_shapes=[
            pltpu.VMEM((count, branches, pieces, each, length), jnp.bfloat16),
            pltpu.VMEM(spectra.shape, spectra.dtype),
            pltpu.VMEM(phases.shape, phases.dtype),
            pltpu.VMEM(shares.shape, shares.dtype),
            pltpu.VMEM((2 * length, 2 * length), jnp.bfloat16),
            pltpu.VMEM((branches, positions, each, length), jnp.float32),
            pltpu.VMEM((blocks * each, 2 * length), jnp.bfloat16),
            pltpu.VMEM((blocks * each, 2 * length), jnp.float32),
            pltpu.VMEM((16, channels), jnp.float32),
            pltpu.VMEM((channels, 16), jnp.float32),
            pltpu.VMEM((count, across, each, wide), jnp.bfloat16),
            pltpu.SemaphoreType.DMA((5,)),
            pltpu.SemaphoreType.DMA((count,)),
        ],
        compiler_params=pltpu.CompilerParams(vmem_limit_bytes=MOST),
    )(mine, came, spectra, phases, shares, taps, skip, edge, *shifted)


def finish_kernel(share, carried_ref, own_ref, weight_ref, *refs):
    came, out_ref = refs[:-1], refs[-1]
    count, across, each, wide = carried_ref.shape
    me = lax.axis_index("tp")
    before = lax.rem(lax.axis_index("seq") + count - 1, count)
    first = (me == 0).astype(jnp.float32)
    lane = lax.broadcasted_iota(jnp.int32, (each, wide), 1)
    pairs = [(own_ref[...], weight_ref[...])] + [(ref[:, :wide], ref[:, wide:]) for ref in came]
    total = jnp.zeros((wide, out_ref.shape[1]), jnp.float32)
    for flip, (gate, weight) in enumerate(pairs):
        source = jnp.bitwise_xor(me, flip)
        edge = carried_ref[before, source].astype(jnp.float32) * first
        edges = [
            jnp.where(lane < 2, pltpu.roll(edge, wide - share - 2 * block, 1), 0.0) for block in range(count)
        ]
        gate = gate.astype(jnp.float32) + jnp.concatenate(edges, axis=0)
        part = carried_ref[:, source].astype(jnp.float32).reshape(count * each, wide)
        total = total + lax.dot_general(
            (part * gate).astype(jnp.bfloat16), weight, (((0,), (0,)), ((), ())), preferred_element_type=jnp.float32
        )
    out_ref[...] = total[:share].astype(jnp.bfloat16)


def finish(carried, own, weight, came, share):
    return pl.pallas_call(
        functools.partial(finish_kernel, share),
        in_specs=[VMEM] * (3 + len(came)),
        out_specs=VMEM,
        out_shape=jax.ShapeDtypeStruct((share, weight.shape[1]), jnp.bfloat16),
        compiler_params=pltpu.CompilerParams(vmem_limit_bytes=LIMIT),
    )(carried, own, weight, *came)


def spread(array, axes):
    return lax.all_to_all(array, axes, split_axis=0, concat_axis=0, tiled=True)


def local(tokens, w_in, short_taps, skip_bias, filter_spectra, w_out):
    count, across = lax.axis_size("seq"), lax.axis_size("tp")
    length = filter_spectra.shape[3]
    spectra = spread(send_spectra(filter_spectra, count), "seq")
    gathered = lax.all_gather(tokens, "tp", axis=0, tiled=True)
    mine, other, edge, own, *windows = project(gathered, w_in, short_taps, skip_bias, count, across, length)
    came = lax.ppermute(other, "seq", [(i, i ^ 1) for i in range(count)])
    onward = relay(mine, came)
    shifted = [
        lax.ppermute(array, "seq", [(i, (i + 2 * shift) % count) for i in range(count)])
        for shift, array in enumerate(onward, 1)
    ]
    packed = [flipped(array, flip, across) for flip, array in enumerate(pack(windows, w_out), 1)]
    carried = convolve(mine, came, shifted, spectra, short_taps, skip_bias, edge, across)
    shape = carried.shape
    carried = spread(carried.reshape((count * across,) + shape[2:]), ("seq", "tp"))
    return finish(carried.reshape(shape), own, w_out, packed, tokens.shape[0])


def solution(mesh):
    in_specs = (
        P(("seq", "tp"), None),
        P(None, None, "tp"),
        P(None, None, "tp"),
        P(None, "tp"),
        P(None, None, "seq", None, "tp"),
        P("tp", None),
    )
    out_specs = P(("seq", "tp"), None)
    return jax.shard_map(local, mesh=mesh, in_specs=in_specs, out_specs=out_specs, check_vma=False)
```

```python
import functools
import math

import jax
import jax.numpy as jnp
import numpy as np
from jax import lax
from jax.experimental import pallas as pl
from jax.experimental.pallas import tpu as pltpu
from jax.sharding import PartitionSpec as P

VMEM = pl.BlockSpec(memory_space=pltpu.VMEM)
ANY = pl.BlockSpec(memory_space=pl.ANY)
MOST = 63 * 1024 * 1024
LANES = 128
HALF_ROOT = math.sqrt(0.75)
LIMIT = 20 * 1024 * 1024


def lanes_table():
    angles = 2.0 * np.pi / LANES * (np.outer(np.arange(LANES), np.arange(LANES)) % LANES)
    cos, sin = np.cos(angles), np.sin(angles)
    return jnp.asarray(np.block([[cos, -sin], [sin, cos]]), jnp.bfloat16)


def twist_rows(bins):
    angles = 2.0 * np.pi / (bins * LANES) * np.outer(np.arange(bins), np.arange(LANES))
    return jnp.asarray(np.concatenate([np.cos(angles), -np.sin(angles)]), jnp.float32)


def window_width(share, count):
    return -(-(share + 2 * count) // LANES) * LANES


def share_table(length, share, wide):
    columns = np.arange(length)
    table = np.zeros((length, length // share * wide))
    table[columns, columns // share * wide + columns % share] = 1.0
    return jnp.asarray(table, jnp.bfloat16)


def times(pair, k, size, direction):
    re, im = pair
    cos, sin = math.cos(2 * math.pi * k / size), direction * math.sin(2 * math.pi * k / size)
    return re * cos - im * sin, re * sin + im * cos


def forward_half(values):
    if len(values) == 1:
        return [(values[0], None), (values[0], None)]
    if len(values) == 3:
        both, gap = values[1] + values[2], values[1] - values[2]
        return [
            (values[0] + both, None),
            (values[0] + 0.5 * gap, -HALF_ROOT * both),
            (values[0] - 0.5 * both, -HALF_ROOT * gap),
            (values[0] - gap, None),
        ]
    even, odd = forward_half(values[0::2]), forward_half(values[1::2])
    half = len(values)
    quarter = half // 2
    out = [None] * (half + 1)
    out[0] = (even[0][0] + odd[0][0], None)
    out[half] = (even[0][0] - odd[0][0], None)
    out[quarter] = (even[quarter][0], -odd[quarter][0])
    for k in range(1, quarter):
        re, im = times(odd[k], k, 2 * half, -1.0)
        out[k] = (even[k][0] + re, even[k][1] + im)
        out[half - k] = (even[k][0] - re, im - even[k][1])
    return out


def inverse_half(bins):
    half = len(bins) - 1
    if half == 1:
        return [bins[0][0] + bins[1][0]]
    if half == 3:
        (zero, _), (re, im), (re_two, im_two), (three, _) = bins
        both, gap = zero + three, zero - three
        return [
            both + 2.0 * (re + re_two),
            gap + (re - re_two) - 2.0 * HALF_ROOT * (im + im_two),
            both - (re + re_two) - 2.0 * HALF_ROOT * (im - im_two),
        ]
    quarter = half // 2
    even = [(bins[0][0] + bins[half][0], None)]
    odd = [(bins[0][0] - bins[half][0], None)]
    for k in range(1, quarter):
        (a, b), (c, d) = bins[k], bins[half - k]
        even.append((a + c, b - d))
        odd.append(times((a - c, b + d), k, 2 * half, 1.0))
    even.append((2.0 * bins[quarter][0], None))
    odd.append((-2.0 * bins[quarter][1], None))
    out = [None] * half
    out[0::2] = inverse_half(even)
    out[1::2] = inverse_half(odd)
    return out


def spectra_kernel(spectra_ref, out_ref, arriving, leaving, sems_in, sems_out):
    orders, parts, residues = spectra_ref.shape[:3]
    count, slabs, each, length = out_ref.shape
    steps, groups = length // LANES, arriving.shape[1]
    fetches, stores = [], []
    for i in range(slabs):
        order, part, residue = i // (parts * residues), i // residues % parts, i % residues
        for group in range(groups):
            source = spectra_ref.at[order, part, residue, :, pl.ds(group * LANES, LANES)]
            fetches.append(pltpu.make_async_copy(source, arriving.at[i, group], sems_in.at[i, group]))
        stores.append(pltpu.make_async_copy(leaving.at[i], out_ref.at[:, i], sems_out.at[i]))
    for fetch in fetches:
        fetch.start()
    some = count // groups
    for i, store in enumerate(stores):
        runs = []
        for group in range(groups):
            fetches[i * groups + group].wait()
            runs.append(jnp.concatenate([arriving[i, group, pl.ds(start, LANES, stride=steps), :] for start in range(steps)], axis=0))
        leaving[i] = jnp.concatenate(runs, axis=1).astype(jnp.bfloat16).T.reshape(count, each, length)
        store.start()
    for store in stores:
        store.wait()


def send_spectra(spectra, count):
    orders, parts, residues, length, channels = spectra.shape
    each = channels // count
    slabs = orders * parts * residues
    return pl.pallas_call(
        spectra_kernel,
        in_specs=[ANY],
        out_specs=ANY,
        out_shape=jax.ShapeDtypeStruct((count, slabs, each, length), jnp.bfloat16),
        scratch_shapes=[
            pltpu.VMEM((slabs, channels // LANES, length, LANES), jnp.float32),
            pltpu.VMEM((slabs, count, each, length), jnp.bfloat16),
            pltpu.SemaphoreType.DMA((slabs, channels // LANES)),
            pltpu.SemaphoreType.DMA((slabs,)),
        ],
        compiler_params=pltpu.CompilerParams(vmem_limit_bytes=MOST),
    )(spectra)


def tap_columns(taps_ref, skip_ref, gathered):
    branches = taps_ref.shape[0]
    for branch in range(branches):
        gathered[branch * 3 : branch * 3 + 3] = taps_ref[branch]
    gathered[9:11] = skip_ref[...]
    return gathered[...].T


def filter_lines(now, last, scale, lane):
    total = scale[0] * now
    rolls = []
    for back in (1, 2):
        rolled = pltpu.roll(now, back, 1)
        total = total + scale[back] * jnp.where(lane < back, last[back - 1], rolled)
        rolls.append(rolled)
    return total, rolls


def project_kernel(tokens_ref, weight_ref, taps_ref, skip_ref, *refs):
    mine_ref, other_ref, edge_ref = refs[:3]
    outs, (held, gathered, windows) = refs[3:-3], refs[-3:]
    count, pieces, each, length = held.shape
    across, channels, wide = windows.shape
    share = pieces * length // across
    branch = pl.program_id(0)
    me = lax.axis_index("seq")
    rows = jnp.dot(tokens_ref[...], weight_ref[0], preferred_element_type=jnp.float32)
    turned = [rows[piece * length : (piece + 1) * length].T for piece in range(pieces)]

    @pl.when(branch < 2)
    def _():
        for piece in range(pieces):
            held[:, piece] = turned[piece].reshape(count, each, length).astype(jnp.bfloat16)
        for shift in range(count // 2):
            to = lax.rem(me + 2 * shift, count)
            mine_ref[shift, 0] = held[to]
            other_ref[shift, 0] = held[jnp.bitwise_xor(to, 1)]

    @pl.when(branch == 2)
    def _():
        columns = tap_columns(taps_ref, skip_ref, gathered)
        scale = [jnp.broadcast_to(columns[:, 6 + i : 7 + i], (channels, length)) for i in range(3)]
        lane = lax.broadcasted_iota(jnp.int32, (channels, length), 1)
        last = [jnp.zeros((channels, length), jnp.float32)] * 2
        windows[...] = jnp.zeros_like(windows)
        for piece in range(pieces):
            now = turned[piece].astype(jnp.bfloat16).astype(jnp.float32)
            total, last = filter_lines(now, last, scale, lane)
            for part in range(length // share):
                window = total[:, part * share : (part + 1) * share]
                windows[piece * (length // share) + part, :, :share] = window.astype(jnp.bfloat16)
        for flip, out in enumerate(outs):
            out[...] = windows[jnp.bitwise_xor(lax.axis_index("tp"), flip)]
        edge = jnp.where(lane < 1, scale[1] * last[0], 0.0) + jnp.where(lane < 2, scale[2] * last[1], 0.0)
        edge = edge[:, :LANES] * (me < count - 1).astype(jnp.float32)
        if wide > LANES:
            edge = jnp.concatenate([edge, jnp.zeros((channels, wide - LANES), jnp.float32)], axis=1)
        total = jnp.zeros((each, wide), jnp.float32)
        for block in range(count):
            total = total + pltpu.roll(edge[block * each : (block + 1) * each], share + 2 * block, 1)
        edge_ref[...] = total.astype(jnp.bfloat16)


def project(tokens, weights, taps, skip, count, across, length):
    rows, depth = tokens.shape
    branches, _, channels = weights.shape
    each, pieces = channels // count, rows // length
    wide = window_width(rows // across, count)
    half = (count // 2, 1, pieces, each, length)
    return pl.pallas_call(
        project_kernel,
        grid=(branches,),
        in_specs=[
            pl.BlockSpec((rows, depth), lambda b: (0, 0)),
            pl.BlockSpec((1, depth, channels), lambda b: (b, 0, 0)),
            pl.BlockSpec(taps.shape, lambda b: (0, 0, 0)),
            pl.BlockSpec(skip.shape, lambda b: (0, 0)),
        ],
        out_specs=[
            pl.BlockSpec(half, lambda b: (0, jnp.minimum(b, 1), 0, 0, 0)),
            pl.BlockSpec(half, lambda b: (0, jnp.minimum(b, 1), 0, 0, 0)),
            pl.BlockSpec((each, wide), lambda b: (0, 0)),
        ]
        + [pl.BlockSpec((channels, wide), lambda b: (0, 0))] * across,
        out_shape=[
            jax.ShapeDtypeStruct((count // 2, 2) + half[2:], jnp.bfloat16),
            jax.ShapeDtypeStruct((count // 2, 2) + half[2:], jnp.bfloat16),
            jax.ShapeDtypeStruct((each, wide), jnp.bfloat16),
        ]
        + [jax.ShapeDtypeStruct((channels, wide), jnp.bfloat16)] * across,
        scratch_shapes=[
            pltpu.VMEM((count, pieces, each, length), jnp.bfloat16),
            pltpu.VMEM((16, channels), jnp.float32),
            pltpu.VMEM((across, channels, wide), jnp.bfloat16),
        ],
        compiler_params=pltpu.CompilerParams(vmem_limit_bytes=LIMIT),
    )(tokens, weights, taps, skip)


def pack_kernel(weight_ref, *refs):
    windows, outs = refs[: len(refs) // 2], refs[len(refs) // 2 :]
    for window, out in zip(windows, outs):
        wide = window.shape[1]
        out[:, :wide] = window[...]
        out[:, wide:] = weight_ref[...]


def pack(windows, weight):
    channels, wide = windows[0].shape
    shape = jax.ShapeDtypeStruct((channels, wide + weight.shape[1]), jnp.bfloat16)
    return pl.pallas_call(
        pack_kernel,
        in_specs=[VMEM] * (1 + len(windows)),
        out_specs=[VMEM] * len(windows),
        out_shape=[shape] * len(windows),
        compiler_params=pltpu.CompilerParams(vmem_limit_bytes=LIMIT),
    )(weight, *windows)


def relay_kernel(mine_ref, came_ref, *outs):
    for shift, out in enumerate(outs, 1):
        out[0] = mine_ref[shift]
        out[1] = came_ref[shift]


def relay(mine, came):
    shape = (2,) + mine.shape[1:]
    return pl.pallas_call(
        relay_kernel,
        in_specs=[VMEM] * 2,
        out_specs=[VMEM] * (mine.shape[0] - 1),
        out_shape=[jax.ShapeDtypeStruct(shape, jnp.bfloat16)] * (mine.shape[0] - 1),
        compiler_params=pltpu.CompilerParams(vmem_limit_bytes=LIMIT),
    )(mine, came)


def forward_tile(values, rows, lines, twist_ref, each):
    count = 2 * len(values)
    bins = forward_half(values)
    for k in range(count):
        cos, sin = twist_ref[k : k + 1], twist_ref[count + k : count + k + 1]
        re, im = bins[min(k, count - k)]
        if im is None:
            pair = (re * cos, re * sin)
        elif 2 * k < count:
            pair = (re * cos - im * sin, re * sin + im * cos)
        else:
            pair = (re * cos + im * sin, re * sin - im * cos)
        at = slice(k * each + rows.start, k * each + rows.stop)
        for part in range(2):
            lines[at, part * LANES : (part + 1) * LANES] = pair[part].astype(jnp.bfloat16)


def respond(spectrum, start, order, spectra_ref, lines, each, blocks):
    residues = spectra_ref.shape[1] // 4
    for k in range(start // each, (start + spectrum.shape[0]) // each):
        at = k * each - start
        re, im = spectrum[at : at + each, :LANES], spectrum[at : at + each, LANES:]
        block, cols = k % blocks, slice(k // blocks * LANES, (k // blocks + 1) * LANES)
        first = order * 2 * residues + block % residues
        gain_re = spectra_ref[block // residues, first, :, cols].astype(jnp.float32)
        gain_im = spectra_ref[block // residues, first + residues, :, cols].astype(jnp.float32)
        lines[k * each : (k + 1) * each, :LANES] = (re * gain_re - im * gain_im).astype(jnp.bfloat16)
        lines[k * each : (k + 1) * each, LANES:] = (-(re * gain_im) - im * gain_re).astype(jnp.bfloat16)


def inverse_tile(wave, rows, twist_ref, half, each):
    count = 2 * half
    turned = []
    for k in range(count):
        cos, sin = twist_ref[k : k + 1], twist_ref[count + k : count + k + 1]
        at = slice(k * each + rows.start, k * each + rows.stop)
        re, im = wave[at, :LANES], wave[at, LANES:]
        turned.append((re * cos - im * sin, re * sin + im * cos))
    bins = [(turned[0][0] * 2.0, None)]
    for k in range(1, half):
        one, two = turned[k], turned[count - k]
        bins.append((one[0] + two[0], two[1] - one[1]))
    bins.append((turned[half][0] * 2.0, None))
    return [value * (0.5 / (count * LANES)) for value in inverse_half(bins)]


def row_steps(total, most):
    step = math.gcd(total, most)
    return [slice(start, start + step) for start in range(0, total, step)]


def flipped(array, flip, size):
    return lax.ppermute(array, "tp", [(i, i ^ flip) for i in range(size)])


def convolve_kernel(*refs):
    mine_in, came_in, spectra_in, twist_in, table_in, shares_in, taps_ref, skip_ref, edge_ref = refs[:9]
    shifted, refs = refs[9:-14], refs[-14:]
    out_ref, held, spectra_ref, twist_ref, table_ref, shares_ref, filtered, lines, wave = refs[:9]
    gathered, columns, leaving, sems, some = refs[9:]
    branches, positions, each, length = filtered.shape
    blocks = 2 * positions
    runs = length // LANES
    count = held.shape[0]
    pieces = positions // count
    slabs = spectra_ref.shape[1]
    me = lax.axis_index("seq")
    other = jnp.bitwise_xor(me, 1)

    inward = [
        pltpu.make_async_copy(mine_in.at[0], held.at[me], some.at[0]),
        pltpu.make_async_copy(came_in.at[0], held.at[other], some.at[1]),
    ]
    for shift, ref in enumerate(shifted, 1):
        for i, one in enumerate((me, other)):
            source = lax.rem(one + count - 2 * shift, count)
            inward.append(pltpu.make_async_copy(ref.at[i], held.at[source], some.at[2 * shift + i]))
    halves = [slice(0, slabs // 2), slice(slabs // 2, slabs)]
    twist = pltpu.make_async_copy(twist_in, twist_ref, sems.at[0])
    table = pltpu.make_async_copy(table_in, table_ref, sems.at[5])
    spectra = [
        pltpu.make_async_copy(spectra_in.at[:, half], spectra_ref.at[:, half], sems.at[1 + i])
        for i, half in enumerate(halves)
    ]
    shares = pltpu.make_async_copy(shares_in, shares_ref, sems.at[3])
    for copy in inward + [twist]:
        copy.start()
    columns[...] = tap_columns(taps_ref, skip_ref, gathered)
    mine = columns[pl.ds(pl.multiple_of(me * each, each), each), :]
    lane = lax.broadcasted_iota(jnp.int32, (each, length), 1)
    for copy in inward:
        copy.wait()
    for copy in [table] + spectra + [shares]:
        copy.start()
    for branch in range(branches):
        last = [jnp.zeros((each, length), jnp.float32)] * 2
        scale = [jnp.broadcast_to(mine[:, branch * 3 + i : branch * 3 + i + 1], (each, length)) for i in range(3)]
        for p in range(positions):
            now = held[p // pieces, branch, p % pieces].astype(jnp.float32)
            filtered[branch, p], last = filter_lines(now, last, scale, lane)
    skips = [jnp.broadcast_to(mine[:, 9 + order : 10 + order], (each, LANES)) for order in range(2)]

    def through(order):
        spectra[order].wait()
        for rows in row_steps(runs * blocks * each, 512):
            spectrum = jnp.dot(lines[rows], table_ref[...], preferred_element_type=jnp.float32)
            respond(spectrum, rows.start, order, spectra_ref, lines, each, blocks)
        for rows in row_steps(runs * blocks * each, 512):
            wave[rows] = jnp.dot(lines[rows], table_ref[...], preferred_element_type=jnp.float32)

    chunk = min(16, each)
    tiles = [slice(row, row + chunk) for row in range(0, each, chunk)]
    places = [(p, slice(run * LANES, (run + 1) * LANES)) for p in range(positions) for run in range(runs)]
    twist.wait()
    for rows in tiles:
        forward_tile([filtered[0, p, rows, cols] for p, cols in places], rows, lines, twist_ref, each)
    table.wait()
    through(0)
    for rows in tiles:
        values = inverse_tile(wave, rows, twist_ref, len(places), each)
        for i, (p, cols) in enumerate(places):
            values[i] = filtered[1, p, rows, cols] * (values[i] + skips[0][rows] * filtered[0, p, rows, cols])
            filtered[0, p, rows, cols] = values[i]
        forward_tile(values, rows, lines, twist_ref, each)
    through(1)
    for rows in tiles:
        values = inverse_tile(wave, rows, twist_ref, len(places), each)
        for value, (p, cols) in zip(values, places):
            filtered[0, p, rows, cols] = value + skips[1][rows] * filtered[0, p, rows, cols]
    shares.wait()
    wide = out_ref.shape[3]
    parts = shares_ref.shape[1] // wide
    flat = filtered[0].reshape(positions * each, length).astype(jnp.bfloat16)
    spread_out = jnp.dot(flat, shares_ref[...], preferred_element_type=jnp.float32)
    for p in range(positions):
        for part in range(parts):
            block = spread_out[p * each : (p + 1) * each, part * wide : (part + 1) * wide]
            leaving[p // pieces, p % pieces * parts + part] = block.astype(jnp.bfloat16)
    following = lax.rem(me + 1, count)
    leaving[following, 0] = leaving[following, 0] + edge_ref[...]
    store = pltpu.make_async_copy(leaving, out_ref, sems.at[4])
    store.start()
    store.wait()


def convolve(mine, came, shifted, spectra, taps, skip, edge, across):
    count, slabs, each, length = spectra.shape
    branches, pieces = mine.shape[1:3]
    positions = count * pieces
    blocks = 2 * positions
    channels = taps.shape[2]
    twist, table = twist_rows(length // LANES * blocks), lanes_table()
    share = pieces * length // across
    wide = window_width(share, count)
    shares = share_table(length, share, wide)
    return pl.pallas_call(
        convolve_kernel,
        in_specs=[ANY] * 6 + [VMEM] * 3 + [ANY] * len(shifted),
        out_specs=ANY,
        out_shape=jax.ShapeDtypeStruct((count, across, each, wide), jnp.bfloat16),
        scratch_shapes=[
            pltpu.VMEM((count, branches, pieces, each, length), jnp.bfloat16),
            pltpu.VMEM(spectra.shape, spectra.dtype),
            pltpu.VMEM(twist.shape, twist.dtype),
            pltpu.VMEM(table.shape, table.dtype),
            pltpu.VMEM(shares.shape, shares.dtype),
            pltpu.VMEM((branches, positions, each, length), jnp.float32),
            pltpu.VMEM((length // LANES * blocks * each, 2 * LANES), jnp.bfloat16),
            pltpu.VMEM((length // LANES * blocks * each, 2 * LANES), jnp.float32),
            pltpu.VMEM((16, channels), jnp.float32),
            pltpu.VMEM((channels, 16), jnp.float32),
            pltpu.VMEM((count, across, each, wide), jnp.bfloat16),
            pltpu.SemaphoreType.DMA((6,)),
            pltpu.SemaphoreType.DMA((count,)),
        ],
        compiler_params=pltpu.CompilerParams(vmem_limit_bytes=56 * 1024 * 1024),
    )(mine, came, spectra, twist, table, shares, taps, skip, edge, *shifted)


def finish_kernel(share, carried_ref, own_ref, weight_ref, *refs):
    came, out_ref = refs[:-1], refs[-1]
    count, across, each, wide = carried_ref.shape
    me = lax.axis_index("tp")
    before = lax.rem(lax.axis_index("seq") + count - 1, count)
    first = (me == 0).astype(jnp.float32)
    lane = lax.broadcasted_iota(jnp.int32, (each, wide), 1)
    pairs = [(own_ref[...], weight_ref[...])] + [(ref[:, :wide], ref[:, wide:]) for ref in came]
    total = jnp.zeros((wide, out_ref.shape[1]), jnp.float32)
    for flip, (gate, weight) in enumerate(pairs):
        source = jnp.bitwise_xor(me, flip)
        edge = carried_ref[before, source].astype(jnp.float32) * first
        edges = [
            jnp.where(lane < 2, pltpu.roll(edge, wide - share - 2 * block, 1), 0.0) for block in range(count)
        ]
        gate = gate.astype(jnp.float32) + jnp.concatenate(edges, axis=0)
        part = carried_ref[:, source].astype(jnp.float32).reshape(count * each, wide)
        total = total + lax.dot_general(
            (part * gate).astype(jnp.bfloat16), weight, (((0,), (0,)), ((), ())), preferred_element_type=jnp.float32
        )
    out_ref[...] = total[:share].astype(jnp.bfloat16)


def finish(carried, own, weight, came, share):
    return pl.pallas_call(
        functools.partial(finish_kernel, share),
        in_specs=[VMEM] * (3 + len(came)),
        out_specs=VMEM,
        out_shape=jax.ShapeDtypeStruct((share, weight.shape[1]), jnp.bfloat16),
        compiler_params=pltpu.CompilerParams(vmem_limit_bytes=LIMIT),
    )(carried, own, weight, *came)


def spread(array, axes):
    return lax.all_to_all(array, axes, split_axis=0, concat_axis=0, tiled=True)


def local(tokens, w_in, short_taps, skip_bias, filter_spectra, w_out):
    count, across = lax.axis_size("seq"), lax.axis_size("tp")
    length = filter_spectra.shape[3]
    spectra = spread(send_spectra(filter_spectra, count), "seq")
    gathered = lax.all_gather(tokens, "tp", axis=0, tiled=True)
    mine, other, edge, own, *windows = project(gathered, w_in, short_taps, skip_bias, count, across, length)
    came = lax.ppermute(other, "seq", [(i, i ^ 1) for i in range(count)])
    onward = relay(mine, came)
    shifted = [
        lax.ppermute(array, "seq", [(i, (i + 2 * shift) % count) for i in range(count)])
        for shift, array in enumerate(onward, 1)
    ]
    packed = [flipped(array, flip, across) for flip, array in enumerate(pack(windows, w_out), 1)]
    carried = convolve(mine, came, shifted, spectra, short_taps, skip_bias, edge, across)
    shape = carried.shape
    carried = spread(carried.reshape((count * across,) + shape[2:]), ("seq", "tp"))
    return finish(carried.reshape(shape), own, w_out, packed, tokens.shape[0])


def solution(mesh):
    in_specs = (
        P(("seq", "tp"), None),
        P(None, None, "tp"),
        P(None, None, "tp"),
        P(None, "tp"),
        P(None, None, "seq", None, "tp"),
        P("tp", None),
    )
    out_specs = P(("seq", "tp"), None)
    return jax.shard_map(local, mesh=mesh, in_specs=in_specs, out_specs=out_specs, check_vma=False)
```

```python
import functools
import math

import jax
import jax.numpy as jnp
import numpy as np
from jax import lax
from jax.experimental import pallas as pl
from jax.experimental.pallas import tpu as pltpu
from jax.sharding import PartitionSpec as P

VMEM = pl.BlockSpec(memory_space=pltpu.VMEM)
ANY = pl.BlockSpec(memory_space=pl.ANY)
MOST = 63 * 1024 * 1024
LANES = 128
HALF_ROOT = math.sqrt(0.75)
LIMIT = 20 * 1024 * 1024


def lanes_waves():
    angles = 2.0 * np.pi / LANES * (np.outer(np.arange(LANES), np.arange(LANES)) % LANES)
    return jnp.asarray(np.stack([np.cos(angles), np.sin(angles)]), jnp.bfloat16)


def fill_tables(waves_ref, table_ref, back_ref):
    cos, sin = waves_ref[0], waves_ref[1]
    for row, parts in enumerate([(cos, -sin, cos, -sin), (sin, cos, -sin, -cos)]):
        for col, part in enumerate(parts):
            table_ref[row * LANES : (row + 1) * LANES, col * LANES : (col + 1) * LANES] = part
    for row, parts in enumerate([(cos, sin), (sin, -cos), (cos, -sin), (sin, cos)]):
        for col, part in enumerate(parts):
            back_ref[row * LANES : (row + 1) * LANES, col * LANES : (col + 1) * LANES] = part


def twist_rows(half):
    angles = np.pi / (half * LANES) * np.outer(np.arange(half + 1), np.arange(LANES))
    return jnp.asarray(np.concatenate([np.cos(angles), -np.sin(angles)]), jnp.float32)


def window_width(share, count):
    return -(-(share + 2 * count) // LANES) * LANES


def fill_shares(shares_ref, share, wide):
    length, columns = shares_ref.shape
    line = lax.broadcasted_iota(jnp.int32, (length, wide), 0)
    lane = lax.broadcasted_iota(jnp.int32, (length, wide), 1)
    for part in range(columns // wide):
        chosen = jnp.logical_and(lane < share, line == lane + part * share)
        shares_ref[:, part * wide : (part + 1) * wide] = chosen.astype(jnp.bfloat16)


def times(pair, k, size, direction):
    re, im = pair
    cos, sin = math.cos(2 * math.pi * k / size), direction * math.sin(2 * math.pi * k / size)
    return re * cos - im * sin, re * sin + im * cos


def forward_half(values):
    if len(values) == 1:
        return [(values[0], None), (values[0], None)]
    if len(values) == 3:
        both, gap = values[1] + values[2], values[1] - values[2]
        return [
            (values[0] + both, None),
            (values[0] + 0.5 * gap, -HALF_ROOT * both),
            (values[0] - 0.5 * both, -HALF_ROOT * gap),
            (values[0] - gap, None),
        ]
    even, odd = forward_half(values[0::2]), forward_half(values[1::2])
    half = len(values)
    quarter = half // 2
    out = [None] * (half + 1)
    out[0] = (even[0][0] + odd[0][0], None)
    out[half] = (even[0][0] - odd[0][0], None)
    out[quarter] = (even[quarter][0], -odd[quarter][0])
    for k in range(1, quarter):
        re, im = times(odd[k], k, 2 * half, -1.0)
        out[k] = (even[k][0] + re, even[k][1] + im)
        out[half - k] = (even[k][0] - re, im - even[k][1])
    return out


def inverse_half(bins):
    half = len(bins) - 1
    if half == 1:
        return [bins[0][0] + bins[1][0]]
    if half == 3:
        (zero, _), (re, im), (re_two, im_two), (three, _) = bins
        both, gap = zero + three, zero - three
        return [
            both + 2.0 * (re + re_two),
            gap + (re - re_two) - 2.0 * HALF_ROOT * (im + im_two),
            both - (re + re_two) - 2.0 * HALF_ROOT * (im - im_two),
        ]
    quarter = half // 2
    even = [(bins[0][0] + bins[half][0], None)]
    odd = [(bins[0][0] - bins[half][0], None)]
    for k in range(1, quarter):
        (a, b), (c, d) = bins[k], bins[half - k]
        even.append((a + c, b - d))
        odd.append(times((a - c, b + d), k, 2 * half, 1.0))
    even.append((2.0 * bins[quarter][0], None))
    odd.append((-2.0 * bins[quarter][1], None))
    out = [None] * half
    out[0::2] = inverse_half(even)
    out[1::2] = inverse_half(odd)
    return out


def spectra_kernel(spectra_ref, out_ref, arriving, leaving, sems_in, sems_out):
    orders, parts, residues = spectra_ref.shape[:3]
    count, slabs, each, length = out_ref.shape
    steps, groups = length // LANES, arriving.shape[1]
    fetches, stores = [], []
    for i in range(slabs):
        order, part, residue = i // (parts * residues), i // residues % parts, i % residues
        for group in range(groups):
            source = spectra_ref.at[order, part, residue, :, pl.ds(group * LANES, LANES)]
            fetches.append(pltpu.make_async_copy(source, arriving.at[i, group], sems_in.at[i, group]))
        stores.append(pltpu.make_async_copy(leaving.at[i], out_ref.at[:, i], sems_out.at[i]))
    for fetch in fetches:
        fetch.start()
    some = count // groups
    for i, store in enumerate(stores):
        runs = []
        for group in range(groups):
            fetches[i * groups + group].wait()
            runs.append(jnp.concatenate([arriving[i, group, pl.ds(start, LANES, stride=steps), :] for start in range(steps)], axis=0))
        leaving[i] = jnp.concatenate(runs, axis=1).astype(jnp.bfloat16).T.reshape(count, each, length)
        store.start()
    for store in stores:
        store.wait()


def send_spectra(spectra, count):
    orders, parts, residues, length, channels = spectra.shape
    each = channels // count
    slabs = orders * parts * residues
    return pl.pallas_call(
        spectra_kernel,
        in_specs=[ANY],
        out_specs=ANY,
        out_shape=jax.ShapeDtypeStruct((count, slabs, each, length), jnp.bfloat16),
        scratch_shapes=[
            pltpu.VMEM((slabs, channels // LANES, length, LANES), jnp.float32),
            pltpu.VMEM((slabs, count, each, length), jnp.bfloat16),
            pltpu.SemaphoreType.DMA((slabs, channels // LANES)),
            pltpu.SemaphoreType.DMA((slabs,)),
        ],
        compiler_params=pltpu.CompilerParams(vmem_limit_bytes=MOST),
    )(spectra)


def tap_columns(taps_ref, skip_ref, gathered):
    branches = taps_ref.shape[0]
    for branch in range(branches):
        gathered[branch * 3 : branch * 3 + 3] = taps_ref[branch]
    gathered[9:11] = skip_ref[...]
    return gathered[...].T


def filter_lines(now, last, scale, lane):
    total = scale[0] * now
    rolls = []
    for back in (1, 2):
        rolled = pltpu.roll(now, back, 1)
        total = total + scale[back] * jnp.where(lane < back, last[back - 1], rolled)
        rolls.append(rolled)
    return total, rolls


def project_kernel(tokens_ref, weight_ref, taps_ref, skip_ref, *refs):
    mine_ref, other_ref, edge_ref = refs[:3]
    outs, (held, gathered, windows) = refs[3:-3], refs[-3:]
    count, pieces, each, length = held.shape
    across, channels, wide = windows.shape
    share = pieces * length // across
    branch = pl.program_id(0)
    me = lax.axis_index("seq")
    rows = jnp.dot(tokens_ref[...], weight_ref[0], preferred_element_type=jnp.float32)
    turned = [rows[piece * length : (piece + 1) * length].T for piece in range(pieces)]

    @pl.when(branch < 2)
    def _():
        for piece in range(pieces):
            held[:, piece] = turned[piece].reshape(count, each, length).astype(jnp.bfloat16)
        for shift in range(count // 2):
            to = lax.rem(me + 2 * shift, count)
            mine_ref[shift, 0] = held[to]
            other_ref[shift, 0] = held[jnp.bitwise_xor(to, 1)]

    @pl.when(branch == 2)
    def _():
        columns = tap_columns(taps_ref, skip_ref, gathered)
        scale = [jnp.broadcast_to(columns[:, 6 + i : 7 + i], (channels, length)) for i in range(3)]
        lane = lax.broadcasted_iota(jnp.int32, (channels, length), 1)
        last = [jnp.zeros((channels, length), jnp.float32)] * 2
        windows[...] = jnp.zeros_like(windows)
        for piece in range(pieces):
            now = turned[piece].astype(jnp.bfloat16).astype(jnp.float32)
            total, last = filter_lines(now, last, scale, lane)
            for part in range(length // share):
                window = total[:, part * share : (part + 1) * share]
                windows[piece * (length // share) + part, :, :share] = window.astype(jnp.bfloat16)
        for flip, out in enumerate(outs):
            out[...] = windows[jnp.bitwise_xor(lax.axis_index("tp"), flip)]
        edge = jnp.where(lane < 1, scale[1] * last[0], 0.0) + jnp.where(lane < 2, scale[2] * last[1], 0.0)
        edge = edge[:, :LANES] * (me < count - 1).astype(jnp.float32)
        if wide > LANES:
            edge = jnp.concatenate([edge, jnp.zeros((channels, wide - LANES), jnp.float32)], axis=1)
        total = jnp.zeros((each, wide), jnp.float32)
        for block in range(count):
            total = total + pltpu.roll(edge[block * each : (block + 1) * each], share + 2 * block, 1)
        edge_ref[...] = total.astype(jnp.bfloat16)


def project(tokens, weights, taps, skip, count, across, length):
    rows, depth = tokens.shape
    branches, _, channels = weights.shape
    each, pieces = channels // count, rows // length
    wide = window_width(rows // across, count)
    half = (count // 2, 1, pieces, each, length)
    return pl.pallas_call(
        project_kernel,
        grid=(branches,),
        in_specs=[
            pl.BlockSpec((rows, depth), lambda b: (0, 0)),
            pl.BlockSpec((1, depth, channels), lambda b: (b, 0, 0)),
            pl.BlockSpec(taps.shape, lambda b: (0, 0, 0)),
            pl.BlockSpec(skip.shape, lambda b: (0, 0)),
        ],
        out_specs=[
            pl.BlockSpec(half, lambda b: (0, jnp.minimum(b, 1), 0, 0, 0)),
            pl.BlockSpec(half, lambda b: (0, jnp.minimum(b, 1), 0, 0, 0)),
            pl.BlockSpec((each, wide), lambda b: (0, 0)),
        ]
        + [pl.BlockSpec((channels, wide), lambda b: (0, 0))] * across,
        out_shape=[
            jax.ShapeDtypeStruct((count // 2, 2) + half[2:], jnp.bfloat16),
            jax.ShapeDtypeStruct((count // 2, 2) + half[2:], jnp.bfloat16),
            jax.ShapeDtypeStruct((each, wide), jnp.bfloat16),
        ]
        + [jax.ShapeDtypeStruct((channels, wide), jnp.bfloat16)] * across,
        scratch_shapes=[
            pltpu.VMEM((count, pieces, each, length), jnp.bfloat16),
            pltpu.VMEM((16, channels), jnp.float32),
            pltpu.VMEM((across, channels, wide), jnp.bfloat16),
        ],
        compiler_params=pltpu.CompilerParams(vmem_limit_bytes=LIMIT),
    )(tokens, weights, taps, skip)


def pack_kernel(weight_ref, *refs):
    windows, outs = refs[: len(refs) // 2], refs[len(refs) // 2 :]
    for window, out in zip(windows, outs):
        wide = window.shape[1]
        out[:, :wide] = window[...]
        out[:, wide:] = weight_ref[...]


def pack(windows, weight):
    channels, wide = windows[0].shape
    shape = jax.ShapeDtypeStruct((channels, wide + weight.shape[1]), jnp.bfloat16)
    return pl.pallas_call(
        pack_kernel,
        in_specs=[VMEM] * (1 + len(windows)),
        out_specs=[VMEM] * len(windows),
        out_shape=[shape] * len(windows),
        compiler_params=pltpu.CompilerParams(vmem_limit_bytes=LIMIT),
    )(weight, *windows)


def relay_kernel(mine_ref, came_ref, *outs):
    for shift, out in enumerate(outs, 1):
        out[0] = mine_ref[shift]
        out[1] = came_ref[shift]


def relay(mine, came):
    shape = (2,) + mine.shape[1:]
    return pl.pallas_call(
        relay_kernel,
        in_specs=[VMEM] * 2,
        out_specs=[VMEM] * (mine.shape[0] - 1),
        out_shape=[jax.ShapeDtypeStruct(shape, jnp.bfloat16)] * (mine.shape[0] - 1),
        compiler_params=pltpu.CompilerParams(vmem_limit_bytes=LIMIT),
    )(mine, came)


def forward_tile(values, rows, lines, twist_ref, each):
    bins = forward_half(values)
    for k, (re, im) in enumerate(bins):
        cos, sin = twist_ref[k : k + 1], twist_ref[len(bins) + k : len(bins) + k + 1]
        pair = (re * cos, re * sin) if im is None else (re * cos - im * sin, re * sin + im * cos)
        at = slice(k * each + rows.start, k * each + rows.stop)
        for part in range(2):
            lines[at, part * LANES : (part + 1) * LANES] = pair[part].astype(jnp.bfloat16)


def respond(spectrum, start, order, spectra_ref, answers, each, blocks, half):
    residues = spectra_ref.shape[1] // 4
    for k in range(start // each, (start + spectrum.shape[0]) // each):
        at = k * each - start
        for mirror in range(2 if 0 < k < half else 1):
            col = 2 * mirror * LANES
            re, im = spectrum[at : at + each, col : col + LANES], spectrum[at : at + each, col + LANES : col + 2 * LANES]
            bin_at = 2 * half - k if mirror else k
            block, cols = bin_at % blocks, slice(bin_at // blocks * LANES, (bin_at // blocks + 1) * LANES)
            first = order * 2 * residues + block % residues
            gain_re = spectra_ref[block // residues, first, :, cols].astype(jnp.float32)
            gain_im = spectra_ref[block // residues, first + residues, :, cols].astype(jnp.float32)
            if mirror:
                gain_re, gain_im = pltpu.roll(gain_re, 1, 1), pltpu.roll(gain_im, 1, 1)
            rows = slice(k * each, (k + 1) * each)
            answers[rows, col : col + LANES] = (re * gain_re - im * gain_im).astype(jnp.bfloat16)
            answers[rows, col + LANES : col + 2 * LANES] = (-(re * gain_im) - im * gain_re).astype(jnp.bfloat16)


def inverse_tile(wave, rows, twist_ref, half, each):
    bins = []
    for k in range(half + 1):
        cos, sin = twist_ref[k : k + 1], twist_ref[half + 1 + k : half + 2 + k]
        at = slice(k * each + rows.start, k * each + rows.stop)
        re, im = wave[at, :LANES], wave[at, LANES:]
        if k in (0, half):
            bins.append((2.0 * (re * cos + im * sin), None))
        else:
            bins.append((re * cos + im * sin, im * cos - re * sin))
    return [value * (0.25 / (half * LANES)) for value in inverse_half(bins)]


def row_steps(total, step):
    return [slice(start, min(start + step, total)) for start in range(0, total, step)]


def flipped(array, flip, size):
    return lax.ppermute(array, "tp", [(i, i ^ flip) for i in range(size)])


def convolve_kernel(*refs):
    mine_in, came_in, spectra_in, twist_ref, waves_ref, taps_ref, skip_ref, edge_ref = refs[:8]
    shifted, refs = refs[8:-14], refs[-14:]
    out_ref, held, spectra_ref, table_ref, back_ref, shares_ref, filtered, lines, answers, wave = refs[:10]
    gathered, columns, leaving, sems = refs[10:]
    branches, positions, each, length = filtered.shape
    blocks = 2 * positions
    runs = length // LANES
    count = held.shape[0]
    pieces = positions // count
    slabs = spectra_ref.shape[1]
    me = lax.axis_index("seq")
    other = jnp.bitwise_xor(me, 1)

    held[me] = mine_in[0]
    held[other] = came_in[0]
    for shift, ref in enumerate(shifted, 1):
        for i, one in enumerate((me, other)):
            held[lax.rem(one + count - 2 * shift, count)] = ref[i]
    halves = [slice(0, slabs // 2), slice(slabs // 2, slabs)]
    spectra = [
        pltpu.make_async_copy(spectra_in.at[:, half], spectra_ref.at[:, half], sems.at[1 + i])
        for i, half in enumerate(halves)
    ]
    for copy in spectra:
        copy.start()
    columns[...] = tap_columns(taps_ref, skip_ref, gathered)
    mine = columns[pl.ds(pl.multiple_of(me * each, each), each), :]
    lane = lax.broadcasted_iota(jnp.int32, (each, length), 1)
    fill_tables(waves_ref, table_ref, back_ref)
    wide = out_ref.shape[3]
    fill_shares(shares_ref, pieces * length // out_ref.shape[1], wide)
    for branch in range(branches):
        last = [jnp.zeros((each, length), jnp.float32)] * 2
        scale = [jnp.broadcast_to(mine[:, branch * 3 + i : branch * 3 + i + 1], (each, length)) for i in range(3)]
        for p in range(positions):
            now = held[p // pieces, branch, p % pieces].astype(jnp.float32)
            filtered[branch, p], last = filter_lines(now, last, scale, lane)
    skips = [jnp.broadcast_to(mine[:, 9 + order : 10 + order], (each, LANES)) for order in range(2)]

    half = runs * positions
    steps = row_steps((half + 1) * each, max(1, 160 // each) * each)
    for k in (0, half):
        answers[k * each : (k + 1) * each, 2 * LANES :] = jnp.zeros((each, 2 * LANES), jnp.bfloat16)

    def through(order):
        spectra[order].wait()
        for rows in steps:
            spectrum = jnp.dot(lines[rows], table_ref[...], preferred_element_type=jnp.float32)
            respond(spectrum, rows.start, order, spectra_ref, answers, each, blocks, half)
        for rows in steps:
            wave[rows] = jnp.dot(answers[rows], back_ref[...], preferred_element_type=jnp.float32)

    chunk = min(16, each)
    tiles = [slice(row, row + chunk) for row in range(0, each, chunk)]
    places = [(p, slice(run * LANES, (run + 1) * LANES)) for p in range(positions) for run in range(runs)]
    for rows in tiles:
        forward_tile([filtered[0, p, rows, cols] for p, cols in places], rows, lines, twist_ref, each)
    through(0)
    for rows in tiles:
        values = inverse_tile(wave, rows, twist_ref, len(places), each)
        for i, (p, cols) in enumerate(places):
            values[i] = filtered[1, p, rows, cols] * (values[i] + skips[0][rows] * filtered[0, p, rows, cols])
            filtered[0, p, rows, cols] = values[i]
        forward_tile(values, rows, lines, twist_ref, each)
    through(1)
    for rows in tiles:
        values = inverse_tile(wave, rows, twist_ref, len(places), each)
        for value, (p, cols) in zip(values, places):
            filtered[0, p, rows, cols] = value + skips[1][rows] * filtered[0, p, rows, cols]
    parts = shares_ref.shape[1] // wide
    following = lax.rem(me + 1, count)
    stores = []
    for i, some_p in enumerate((range(positions // 2), range(positions // 2, positions))):
        flat = filtered[0, some_p.start : some_p.stop].reshape(len(some_p) * each, length).astype(jnp.bfloat16)
        spread_out = jnp.dot(flat, shares_ref[...], preferred_element_type=jnp.float32)
        for at, p in enumerate(some_p):
            for part in range(parts):
                block = spread_out[at * each : (at + 1) * each, part * wide : (part + 1) * wide]
                leaving[p // pieces, p % pieces * parts + part] = block.astype(jnp.bfloat16)
        half_count = slice(some_p.start // pieces, some_p.stop // pieces)
        here = jnp.logical_and(following >= half_count.start, following < half_count.stop)

        @pl.when(here)
        def _():
            leaving[following, 0] = leaving[following, 0] + edge_ref[...]

        stores.append(pltpu.make_async_copy(leaving.at[half_count], out_ref.at[half_count], sems.at[2 + i]))
        stores[-1].start()
    for store in stores:
        store.wait()


def convolve(mine, came, shifted, spectra, taps, skip, edge, across):
    count, slabs, each, length = spectra.shape
    branches, pieces = mine.shape[1:3]
    positions = count * pieces
    blocks = 2 * positions
    channels = taps.shape[2]
    half = length // LANES * positions
    twist, waves = twist_rows(half), lanes_waves()
    share = pieces * length // across
    wide = window_width(share, count)
    return pl.pallas_call(
        convolve_kernel,
        in_specs=[VMEM] * 2 + [ANY] + [VMEM] * 5 + [VMEM] * len(shifted),
        out_specs=ANY,
        out_shape=jax.ShapeDtypeStruct((count, across, each, wide), jnp.bfloat16),
        scratch_shapes=[
            pltpu.VMEM((count, branches, pieces, each, length), jnp.bfloat16),
            pltpu.VMEM(spectra.shape, spectra.dtype),
            pltpu.VMEM((2 * LANES, 4 * LANES), jnp.bfloat16),
            pltpu.VMEM((4 * LANES, 2 * LANES), jnp.bfloat16),
            pltpu.VMEM((length, length // share * wide), jnp.bfloat16),
            pltpu.VMEM((branches, positions, each, length), jnp.float32),
            pltpu.VMEM(((half + 1) * each, 2 * LANES), jnp.bfloat16),
            pltpu.VMEM(((half + 1) * each, 4 * LANES), jnp.bfloat16),
            pltpu.VMEM(((half + 1) * each, 2 * LANES), jnp.float32),
            pltpu.VMEM((16, channels), jnp.float32),
            pltpu.VMEM((channels, 16), jnp.float32),
            pltpu.VMEM((count, across, each, wide), jnp.bfloat16),
            pltpu.SemaphoreType.DMA((4,)),
        ],
        compiler_params=pltpu.CompilerParams(vmem_limit_bytes=52 * 1024 * 1024),
    )(mine, came, spectra, twist, waves, taps, skip, edge, *shifted)


def finish_kernel(share, carried_ref, own_ref, weight_ref, *refs):
    came, out_ref = refs[:-1], refs[-1]
    count, across, each, wide = carried_ref.shape
    me = lax.axis_index("tp")
    before = lax.rem(lax.axis_index("seq") + count - 1, count)
    first = (me == 0).astype(jnp.float32)
    lane = lax.broadcasted_iota(jnp.int32, (each, wide), 1)
    pairs = [(own_ref[...], weight_ref[...])] + [(ref[:, :wide], ref[:, wide:]) for ref in came]
    total = jnp.zeros((wide, out_ref.shape[1]), jnp.float32)
    for flip, (gate, weight) in enumerate(pairs):
        source = jnp.bitwise_xor(me, flip)
        edge = carried_ref[before, source].astype(jnp.float32) * first
        edges = [
            jnp.where(lane < 2, pltpu.roll(edge, wide - share - 2 * block, 1), 0.0) for block in range(count)
        ]
        gate = gate.astype(jnp.float32) + jnp.concatenate(edges, axis=0)
        part = carried_ref[:, source].astype(jnp.float32).reshape(count * each, wide)
        total = total + lax.dot_general(
            (part * gate).astype(jnp.bfloat16), weight, (((0,), (0,)), ((), ())), preferred_element_type=jnp.float32
        )
    out_ref[...] = total[:share].astype(jnp.bfloat16)


def finish(carried, own, weight, came, share):
    return pl.pallas_call(
        functools.partial(finish_kernel, share),
        in_specs=[VMEM] * (3 + len(came)),
        out_specs=VMEM,
        out_shape=jax.ShapeDtypeStruct((share, weight.shape[1]), jnp.bfloat16),
        compiler_params=pltpu.CompilerParams(vmem_limit_bytes=LIMIT),
    )(carried, own, weight, *came)


def spread(array, axes):
    return lax.all_to_all(array, axes, split_axis=0, concat_axis=0, tiled=True)


def local(tokens, w_in, short_taps, skip_bias, filter_spectra, w_out):
    count, across = lax.axis_size("seq"), lax.axis_size("tp")
    length = filter_spectra.shape[3]
    spectra = spread(send_spectra(filter_spectra, count), "seq")
    gathered = lax.all_gather(tokens, "tp", axis=0, tiled=True)
    mine, other, edge, own, *windows = project(gathered, w_in, short_taps, skip_bias, count, across, length)
    came = lax.ppermute(other, "seq", [(i, i ^ 1) for i in range(count)])
    onward = relay(mine, came)
    shifted = [
        lax.ppermute(array, "seq", [(i, (i + 2 * shift) % count) for i in range(count)])
        for shift, array in enumerate(onward, 1)
    ]
    packed = [flipped(array, flip, across) for flip, array in enumerate(pack(windows, w_out), 1)]
    carried = convolve(mine, came, shifted, spectra, short_taps, skip_bias, edge, across)
    shape = carried.shape
    carried = spread(carried.reshape((count * across,) + shape[2:]), ("seq", "tp"))
    return finish(carried.reshape(shape), own, w_out, packed, tokens.shape[0])


def solution(mesh):
    in_specs = (
        P(("seq", "tp"), None),
        P(None, None, "tp"),
        P(None, None, "tp"),
        P(None, "tp"),
        P(None, None, "seq", None, "tp"),
        P("tp", None),
    )
    out_specs = P(("seq", "tp"), None)
    return jax.shard_map(local, mesh=mesh, in_specs=in_specs, out_specs=out_specs, check_vma=False)
```

```python
import functools
import math

import jax
import jax.numpy as jnp
import numpy as np
from jax import lax
from jax.experimental import pallas as pl
from jax.experimental.pallas import tpu as pltpu
from jax.sharding import PartitionSpec as P

VMEM = pl.BlockSpec(memory_space=pltpu.VMEM)
ANY = pl.BlockSpec(memory_space=pl.ANY)
MOST = 63 * 1024 * 1024
LANES = 128
HALF_ROOT = math.sqrt(0.75)
LIMIT = 20 * 1024 * 1024


def lanes_waves():
    angles = 2.0 * np.pi / LANES * (np.outer(np.arange(LANES), np.arange(LANES)) % LANES)
    return jnp.asarray(np.stack([np.cos(angles), np.sin(angles)]), jnp.bfloat16)


def fill_tables(waves_ref, table_ref, back_ref):
    cos, sin = waves_ref[0], waves_ref[1]
    for row, parts in enumerate([(cos, -sin, cos, -sin), (sin, cos, -sin, -cos)]):
        for col, part in enumerate(parts):
            table_ref[row * LANES : (row + 1) * LANES, col * LANES : (col + 1) * LANES] = part
    for row, parts in enumerate([(cos, sin), (sin, -cos), (cos, -sin), (sin, cos)]):
        for col, part in enumerate(parts):
            back_ref[row * LANES : (row + 1) * LANES, col * LANES : (col + 1) * LANES] = part


def twist_rows(half):
    angles = np.pi / (half * LANES) * np.outer(np.arange(half + 1), np.arange(LANES))
    return jnp.asarray(np.concatenate([np.cos(angles), -np.sin(angles)]), jnp.float32)


def window_width(share, count):
    return -(-(share + 2 * count) // LANES) * LANES


def fill_shares(shares_ref, share, wide):
    length, columns = shares_ref.shape
    line = lax.broadcasted_iota(jnp.int32, (length, wide), 0)
    lane = lax.broadcasted_iota(jnp.int32, (length, wide), 1)
    for part in range(columns // wide):
        chosen = jnp.logical_and(lane < share, line == lane + part * share)
        shares_ref[:, part * wide : (part + 1) * wide] = chosen.astype(jnp.bfloat16)


def times(pair, k, size, direction):
    re, im = pair
    cos, sin = math.cos(2 * math.pi * k / size), direction * math.sin(2 * math.pi * k / size)
    return re * cos - im * sin, re * sin + im * cos


def forward_half(values):
    if len(values) == 1:
        return [(values[0], None), (values[0], None)]
    if len(values) == 3:
        both, gap = values[1] + values[2], values[1] - values[2]
        return [
            (values[0] + both, None),
            (values[0] + 0.5 * gap, -HALF_ROOT * both),
            (values[0] - 0.5 * both, -HALF_ROOT * gap),
            (values[0] - gap, None),
        ]
    even, odd = forward_half(values[0::2]), forward_half(values[1::2])
    half = len(values)
    quarter = half // 2
    out = [None] * (half + 1)
    out[0] = (even[0][0] + odd[0][0], None)
    out[half] = (even[0][0] - odd[0][0], None)
    out[quarter] = (even[quarter][0], -odd[quarter][0])
    for k in range(1, quarter):
        re, im = times(odd[k], k, 2 * half, -1.0)
        out[k] = (even[k][0] + re, even[k][1] + im)
        out[half - k] = (even[k][0] - re, im - even[k][1])
    return out


def inverse_half(bins):
    half = len(bins) - 1
    if half == 1:
        return [bins[0][0] + bins[1][0]]
    if half == 3:
        (zero, _), (re, im), (re_two, im_two), (three, _) = bins
        both, gap = zero + three, zero - three
        return [
            both + 2.0 * (re + re_two),
            gap + (re - re_two) - 2.0 * HALF_ROOT * (im + im_two),
            both - (re + re_two) - 2.0 * HALF_ROOT * (im - im_two),
        ]
    quarter = half // 2
    even = [(bins[0][0] + bins[half][0], None)]
    odd = [(bins[0][0] - bins[half][0], None)]
    for k in range(1, quarter):
        (a, b), (c, d) = bins[k], bins[half - k]
        even.append((a + c, b - d))
        odd.append(times((a - c, b + d), k, 2 * half, 1.0))
    even.append((2.0 * bins[quarter][0], None))
    odd.append((-2.0 * bins[quarter][1], None))
    out = [None] * half
    out[0::2] = inverse_half(even)
    out[1::2] = inverse_half(odd)
    return out


def spectra_kernel(spectra_ref, out_ref, arriving, leaving, sems_in, sems_out):
    orders, parts, residues = spectra_ref.shape[:3]
    count, slabs, each, length = out_ref.shape
    steps, groups = length // LANES, arriving.shape[1]
    fetches, stores = [], []
    for i in range(slabs):
        order, part, residue = i // (parts * residues), i // residues % parts, i % residues
        for group in range(groups):
            source = spectra_ref.at[order, part, residue, :, pl.ds(group * LANES, LANES)]
            fetches.append(pltpu.make_async_copy(source, arriving.at[i, group], sems_in.at[i, group]))
        stores.append(pltpu.make_async_copy(leaving.at[i], out_ref.at[:, i], sems_out.at[i]))
    for fetch in fetches:
        fetch.start()
    some = count // groups
    for i, store in enumerate(stores):
        runs = []
        for group in range(groups):
            fetches[i * groups + group].wait()
            runs.append(jnp.concatenate([arriving[i, group, pl.ds(start, LANES, stride=steps), :] for start in range(steps)], axis=0))
        leaving[i] = jnp.concatenate(runs, axis=1).astype(jnp.bfloat16).T.reshape(count, each, length)
        store.start()
    for store in stores:
        store.wait()


def send_spectra(spectra, count):
    orders, parts, residues, length, channels = spectra.shape
    each = channels // count
    slabs = orders * parts * residues
    return pl.pallas_call(
        spectra_kernel,
        in_specs=[ANY],
        out_specs=ANY,
        out_shape=jax.ShapeDtypeStruct((count, slabs, each, length), jnp.bfloat16),
        scratch_shapes=[
            pltpu.VMEM((slabs, channels // LANES, length, LANES), jnp.float32),
            pltpu.VMEM((slabs, count, each, length), jnp.bfloat16),
            pltpu.SemaphoreType.DMA((slabs, channels // LANES)),
            pltpu.SemaphoreType.DMA((slabs,)),
        ],
        compiler_params=pltpu.CompilerParams(vmem_limit_bytes=MOST),
    )(spectra)


def tap_columns(taps_ref, skip_ref, gathered):
    branches = taps_ref.shape[0]
    for branch in range(branches):
        gathered[branch * 3 : branch * 3 + 3] = taps_ref[branch]
    gathered[9:11] = skip_ref[...]
    return gathered[...].T


def filter_lines(now, last, scale, lane):
    total = scale[0] * now
    rolls = []
    for back in (1, 2):
        rolled = pltpu.roll(now, back, 1)
        total = total + scale[back] * jnp.where(lane < back, last[back - 1], rolled)
        rolls.append(rolled)
    return total, rolls


def project_kernel(tokens_ref, weight_ref, taps_ref, skip_ref, *refs):
    mine_ref, other_ref, edge_ref = refs[:3]
    outs, (held, gathered, windows) = refs[3:-3], refs[-3:]
    count, pieces, each, length = held.shape
    across, channels, wide = windows.shape
    share = pieces * length // across
    branch = pl.program_id(0)
    me = lax.axis_index("seq")
    rows = jnp.dot(tokens_ref[...], weight_ref[0], preferred_element_type=jnp.float32)
    turned = [rows[piece * length : (piece + 1) * length].T for piece in range(pieces)]

    @pl.when(branch < 2)
    def _():
        for piece in range(pieces):
            held[:, piece] = turned[piece].reshape(count, each, length).astype(jnp.bfloat16)
        for shift in range(count // 2):
            to = lax.rem(me + 2 * shift, count)
            mine_ref[shift, 0] = held[to]
            other_ref[shift, 0] = held[jnp.bitwise_xor(to, 1)]

    @pl.when(branch == 2)
    def _():
        columns = tap_columns(taps_ref, skip_ref, gathered)
        scale = [jnp.broadcast_to(columns[:, 6 + i : 7 + i], (channels, length)) for i in range(3)]
        lane = lax.broadcasted_iota(jnp.int32, (channels, length), 1)
        last = [jnp.zeros((channels, length), jnp.float32)] * 2
        windows[...] = jnp.zeros_like(windows)
        for piece in range(pieces):
            now = turned[piece].astype(jnp.bfloat16).astype(jnp.float32)
            total, last = filter_lines(now, last, scale, lane)
            for part in range(length // share):
                window = total[:, part * share : (part + 1) * share]
                windows[piece * (length // share) + part, :, :share] = window.astype(jnp.bfloat16)
        for flip, out in enumerate(outs):
            out[...] = windows[jnp.bitwise_xor(lax.axis_index("tp"), flip)]
        edge = jnp.where(lane < 1, scale[1] * last[0], 0.0) + jnp.where(lane < 2, scale[2] * last[1], 0.0)
        edge = edge[:, :LANES] * (me < count - 1).astype(jnp.float32)
        if wide > LANES:
            edge = jnp.concatenate([edge, jnp.zeros((channels, wide - LANES), jnp.float32)], axis=1)
        total = jnp.zeros((each, wide), jnp.float32)
        for block in range(count):
            total = total + pltpu.roll(edge[block * each : (block + 1) * each], share + 2 * block, 1)
        edge_ref[...] = total.astype(jnp.bfloat16)


def project(tokens, weights, taps, skip, count, across, length):
    rows, depth = tokens.shape
    branches, _, channels = weights.shape
    each, pieces = channels // count, rows // length
    wide = window_width(rows // across, count)
    half = (count // 2, 1, pieces, each, length)
    return pl.pallas_call(
        project_kernel,
        grid=(branches,),
        in_specs=[
            pl.BlockSpec((rows, depth), lambda b: (0, 0)),
            pl.BlockSpec((1, depth, channels), lambda b: (b, 0, 0)),
            pl.BlockSpec(taps.shape, lambda b: (0, 0, 0)),
            pl.BlockSpec(skip.shape, lambda b: (0, 0)),
        ],
        out_specs=[
            pl.BlockSpec(half, lambda b: (0, jnp.minimum(b, 1), 0, 0, 0)),
            pl.BlockSpec(half, lambda b: (0, jnp.minimum(b, 1), 0, 0, 0)),
            pl.BlockSpec((each, wide), lambda b: (0, 0)),
        ]
        + [pl.BlockSpec((channels, wide), lambda b: (0, 0))] * across,
        out_shape=[
            jax.ShapeDtypeStruct((count // 2, 2) + half[2:], jnp.bfloat16),
            jax.ShapeDtypeStruct((count // 2, 2) + half[2:], jnp.bfloat16),
            jax.ShapeDtypeStruct((each, wide), jnp.bfloat16),
        ]
        + [jax.ShapeDtypeStruct((channels, wide), jnp.bfloat16)] * across,
        scratch_shapes=[
            pltpu.VMEM((count, pieces, each, length), jnp.bfloat16),
            pltpu.VMEM((16, channels), jnp.float32),
            pltpu.VMEM((across, channels, wide), jnp.bfloat16),
        ],
        compiler_params=pltpu.CompilerParams(vmem_limit_bytes=LIMIT),
    )(tokens, weights, taps, skip)


def pack_kernel(weight_ref, *refs):
    windows, outs = refs[: len(refs) // 2], refs[len(refs) // 2 :]
    for window, out in zip(windows, outs):
        wide = window.shape[1]
        out[:, :wide] = window[...]
        out[:, wide:] = weight_ref[...]


def pack(windows, weight):
    channels, wide = windows[0].shape
    shape = jax.ShapeDtypeStruct((channels, wide + weight.shape[1]), jnp.bfloat16)
    return pl.pallas_call(
        pack_kernel,
        in_specs=[VMEM] * (1 + len(windows)),
        out_specs=[VMEM] * len(windows),
        out_shape=[shape] * len(windows),
        compiler_params=pltpu.CompilerParams(vmem_limit_bytes=LIMIT),
    )(weight, *windows)


def relay_kernel(mine_ref, came_ref, *outs):
    for shift, out in enumerate(outs, 1):
        out[0] = mine_ref[shift]
        out[1] = came_ref[shift]


def relay(mine, came):
    shape = (2,) + mine.shape[1:]
    return pl.pallas_call(
        relay_kernel,
        in_specs=[VMEM] * 2,
        out_specs=[VMEM] * (mine.shape[0] - 1),
        out_shape=[jax.ShapeDtypeStruct(shape, jnp.bfloat16)] * (mine.shape[0] - 1),
        compiler_params=pltpu.CompilerParams(vmem_limit_bytes=LIMIT),
    )(mine, came)


def forward_tile(values, rows, lines, twist_ref, each):
    bins = forward_half(values)
    for k, (re, im) in enumerate(bins):
        cos, sin = twist_ref[k : k + 1], twist_ref[len(bins) + k : len(bins) + k + 1]
        pair = (re * cos, re * sin) if im is None else (re * cos - im * sin, re * sin + im * cos)
        at = slice(k * each + rows.start, k * each + rows.stop)
        for part in range(2):
            lines[at, part * LANES : (part + 1) * LANES] = pair[part].astype(jnp.bfloat16)


def respond(spectrum, start, order, spectra_ref, answers, each, blocks, half):
    residues = spectra_ref.shape[1] // 4
    for k in range(start // each, (start + spectrum.shape[0]) // each):
        at = k * each - start
        for mirror in range(2 if 0 < k < half else 1):
            col = 2 * mirror * LANES
            re, im = spectrum[at : at + each, col : col + LANES], spectrum[at : at + each, col + LANES : col + 2 * LANES]
            bin_at = 2 * half - k if mirror else k
            block, cols = bin_at % blocks, slice(bin_at // blocks * LANES, (bin_at // blocks + 1) * LANES)
            first = order * 2 * residues + block % residues
            gain_re = spectra_ref[block // residues, first, :, cols].astype(jnp.float32)
            gain_im = spectra_ref[block // residues, first + residues, :, cols].astype(jnp.float32)
            if mirror:
                gain_re, gain_im = pltpu.roll(gain_re, 1, 1), pltpu.roll(gain_im, 1, 1)
            rows = slice(k * each, (k + 1) * each)
            answers[rows, col : col + LANES] = (re * gain_re - im * gain_im).astype(jnp.bfloat16)
            answers[rows, col + LANES : col + 2 * LANES] = (-(re * gain_im) - im * gain_re).astype(jnp.bfloat16)


def inverse_tile(wave, rows, twist_ref, half, each):
    bins = []
    for k in range(half + 1):
        cos, sin = twist_ref[k : k + 1], twist_ref[half + 1 + k : half + 2 + k]
        at = slice(k * each + rows.start, k * each + rows.stop)
        re, im = wave[at, :LANES], wave[at, LANES:]
        if k in (0, half):
            bins.append((2.0 * (re * cos + im * sin), None))
        else:
            bins.append((re * cos + im * sin, im * cos - re * sin))
    return [value * (0.25 / (half * LANES)) for value in inverse_half(bins)]


def row_steps(total, step):
    return [slice(start, min(start + step, total)) for start in range(0, total, step)]


def flipped(array, flip, size):
    return lax.ppermute(array, "tp", [(i, i ^ flip) for i in range(size)])


def convolve_kernel(*refs):
    mine_in, came_in, spectra_in, twist_ref, waves_ref, taps_ref, skip_ref, edge_ref = refs[:8]
    shifted, refs = refs[8:-13], refs[-13:]
    out_ref, held, spectra_ref, table_ref, back_ref, shares_ref, filtered, lines, answers, wave = refs[:10]
    gathered, columns, sems = refs[10:]
    branches, positions, each, length = filtered.shape
    blocks = 2 * positions
    runs = length // LANES
    count = held.shape[0]
    pieces = positions // count
    slabs = spectra_ref.shape[1]
    me = lax.axis_index("seq")
    other = jnp.bitwise_xor(me, 1)

    held[me] = mine_in[0]
    held[other] = came_in[0]
    for shift, ref in enumerate(shifted, 1):
        for i, one in enumerate((me, other)):
            held[lax.rem(one + count - 2 * shift, count)] = ref[i]
    halves = [slice(0, slabs // 2), slice(slabs // 2, slabs)]
    spectra = [
        pltpu.make_async_copy(spectra_in.at[:, half], spectra_ref.at[:, half], sems.at[1 + i])
        for i, half in enumerate(halves)
    ]
    for copy in spectra:
        copy.start()
    columns[...] = tap_columns(taps_ref, skip_ref, gathered)
    mine = columns[pl.ds(pl.multiple_of(me * each, each), each), :]
    lane = lax.broadcasted_iota(jnp.int32, (each, length), 1)
    fill_tables(waves_ref, table_ref, back_ref)
    wide = out_ref.shape[3]
    fill_shares(shares_ref, pieces * length // out_ref.shape[1], wide)
    for branch in range(branches):
        last = [jnp.zeros((each, length), jnp.float32)] * 2
        scale = [jnp.broadcast_to(mine[:, branch * 3 + i : branch * 3 + i + 1], (each, length)) for i in range(3)]
        for p in range(positions):
            now = held[p // pieces, branch, p % pieces].astype(jnp.float32)
            filtered[branch, p], last = filter_lines(now, last, scale, lane)
    skips = [jnp.broadcast_to(mine[:, 9 + order : 10 + order], (each, LANES)) for order in range(2)]

    half = runs * positions
    steps = row_steps((half + 1) * each, max(1, 160 // each) * each)
    for k in (0, half):
        answers[k * each : (k + 1) * each, 2 * LANES :] = jnp.zeros((each, 2 * LANES), jnp.bfloat16)

    def through(order):
        spectra[order].wait()
        for rows in steps:
            spectrum = jnp.dot(lines[rows], table_ref[...], preferred_element_type=jnp.float32)
            respond(spectrum, rows.start, order, spectra_ref, answers, each, blocks, half)
        for rows in steps:
            wave[rows] = jnp.dot(answers[rows], back_ref[...], preferred_element_type=jnp.float32)

    chunk = min(16, each)
    tiles = [slice(row, row + chunk) for row in range(0, each, chunk)]
    places = [(p, slice(run * LANES, (run + 1) * LANES)) for p in range(positions) for run in range(runs)]
    for rows in tiles:
        forward_tile([filtered[0, p, rows, cols] for p, cols in places], rows, lines, twist_ref, each)
    through(0)
    for rows in tiles:
        values = inverse_tile(wave, rows, twist_ref, len(places), each)
        for i, (p, cols) in enumerate(places):
            values[i] = filtered[1, p, rows, cols] * (values[i] + skips[0][rows] * filtered[0, p, rows, cols])
            filtered[0, p, rows, cols] = values[i]
        forward_tile(values, rows, lines, twist_ref, each)
    through(1)
    for rows in tiles:
        values = inverse_tile(wave, rows, twist_ref, len(places), each)
        for value, (p, cols) in zip(values, places):
            filtered[0, p, rows, cols] = value + skips[1][rows] * filtered[0, p, rows, cols]
    parts = shares_ref.shape[1] // wide
    following = lax.rem(me + 1, count)
    leaving = out_ref
    for some_p in (range(positions // 2), range(positions // 2, positions)):
        flat = filtered[0, some_p.start : some_p.stop].reshape(len(some_p) * each, length).astype(jnp.bfloat16)
        spread_out = jnp.dot(flat, shares_ref[...], preferred_element_type=jnp.float32)
        for at, p in enumerate(some_p):
            for part in range(parts):
                block = spread_out[at * each : (at + 1) * each, part * wide : (part + 1) * wide]
                leaving[p // pieces, p % pieces * parts + part] = block.astype(jnp.bfloat16)
        half_count = slice(some_p.start // pieces, some_p.stop // pieces)
        here = jnp.logical_and(following >= half_count.start, following < half_count.stop)

        @pl.when(here)
        def _():
            leaving[following, 0] = leaving[following, 0] + edge_ref[...]


def convolve(mine, came, shifted, spectra, taps, skip, edge, across):
    count, slabs, each, length = spectra.shape
    branches, pieces = mine.shape[1:3]
    positions = count * pieces
    blocks = 2 * positions
    channels = taps.shape[2]
    half = length // LANES * positions
    twist, waves = twist_rows(half), lanes_waves()
    share = pieces * length // across
    wide = window_width(share, count)
    return pl.pallas_call(
        convolve_kernel,
        in_specs=[VMEM] * 2 + [ANY] + [VMEM] * 5 + [VMEM] * len(shifted),
        out_specs=VMEM,
        out_shape=jax.ShapeDtypeStruct((count, across, each, wide), jnp.bfloat16),
        scratch_shapes=[
            pltpu.VMEM((count, branches, pieces, each, length), jnp.bfloat16),
            pltpu.VMEM(spectra.shape, spectra.dtype),
            pltpu.VMEM((2 * LANES, 4 * LANES), jnp.bfloat16),
            pltpu.VMEM((4 * LANES, 2 * LANES), jnp.bfloat16),
            pltpu.VMEM((length, length // share * wide), jnp.bfloat16),
            pltpu.VMEM((branches, positions, each, length), jnp.float32),
            pltpu.VMEM(((half + 1) * each, 2 * LANES), jnp.bfloat16),
            pltpu.VMEM(((half + 1) * each, 4 * LANES), jnp.bfloat16),
            pltpu.VMEM(((half + 1) * each, 2 * LANES), jnp.float32),
            pltpu.VMEM((16, channels), jnp.float32),
            pltpu.VMEM((channels, 16), jnp.float32),
            pltpu.SemaphoreType.DMA((4,)),
        ],
        compiler_params=pltpu.CompilerParams(vmem_limit_bytes=52 * 1024 * 1024),
    )(mine, came, spectra, twist, waves, taps, skip, edge, *shifted)


def finish_kernel(share, carried_ref, own_ref, weight_ref, *refs):
    came, out_ref = refs[:-1], refs[-1]
    count, across, each, wide = carried_ref.shape
    me = lax.axis_index("tp")
    before = lax.rem(lax.axis_index("seq") + count - 1, count)
    first = (me == 0).astype(jnp.float32)
    lane = lax.broadcasted_iota(jnp.int32, (each, wide), 1)
    pairs = [(own_ref[...], weight_ref[...])] + [(ref[:, :wide], ref[:, wide:]) for ref in came]
    total = jnp.zeros((wide, out_ref.shape[1]), jnp.float32)
    for flip, (gate, weight) in enumerate(pairs):
        source = jnp.bitwise_xor(me, flip)
        edge = carried_ref[before, source].astype(jnp.float32) * first
        edges = [
            jnp.where(lane < 2, pltpu.roll(edge, wide - share - 2 * block, 1), 0.0) for block in range(count)
        ]
        gate = gate.astype(jnp.float32) + jnp.concatenate(edges, axis=0)
        part = carried_ref[:, source].astype(jnp.float32).reshape(count * each, wide)
        total = total + lax.dot_general(
            (part * gate).astype(jnp.bfloat16), weight, (((0,), (0,)), ((), ())), preferred_element_type=jnp.float32
        )
    out_ref[...] = total[:share].astype(jnp.bfloat16)


def finish(carried, own, weight, came, share):
    return pl.pallas_call(
        functools.partial(finish_kernel, share),
        in_specs=[VMEM] * (3 + len(came)),
        out_specs=VMEM,
        out_shape=jax.ShapeDtypeStruct((share, weight.shape[1]), jnp.bfloat16),
        compiler_params=pltpu.CompilerParams(vmem_limit_bytes=LIMIT),
    )(carried, own, weight, *came)


def spread(array, axes):
    return lax.all_to_all(array, axes, split_axis=0, concat_axis=0, tiled=True)


def local(tokens, w_in, short_taps, skip_bias, filter_spectra, w_out):
    count, across = lax.axis_size("seq"), lax.axis_size("tp")
    length = filter_spectra.shape[3]
    spectra = spread(send_spectra(filter_spectra, count), "seq")
    gathered = lax.all_gather(tokens, "tp", axis=0, tiled=True)
    mine, other, edge, own, *windows = project(gathered, w_in, short_taps, skip_bias, count, across, length)
    came = lax.ppermute(other, "seq", [(i, i ^ 1) for i in range(count)])
    came, *packed = lax.optimization_barrier((came, *pack(windows, w_out)))
    onward = relay(mine, came)
    shifted = [
        lax.ppermute(array, "seq", [(i, (i + 2 * shift) % count) for i in range(count)])
        for shift, array in enumerate(onward, 1)
    ]
    packed = [flipped(array, flip, across) for flip, array in enumerate(packed, 1)]
    carried = convolve(mine, came, shifted, spectra, short_taps, skip_bias, edge, across)
    shape = carried.shape
    carried = spread(carried.reshape((count * across,) + shape[2:]), ("seq", "tp"))
    return finish(carried.reshape(shape), own, w_out, packed, tokens.shape[0])


def solution(mesh):
    in_specs = (
        P(("seq", "tp"), None),
        P(None, None, "tp"),
        P(None, None, "tp"),
        P(None, "tp"),
        P(None, None, "seq", None, "tp"),
        P("tp", None),
    )
    out_specs = P(("seq", "tp"), None)
    return jax.shard_map(local, mesh=mesh, in_specs=in_specs, out_specs=out_specs, check_vma=False)
```

```python
import functools
import math

import jax
import jax.numpy as jnp
import numpy as np
from jax import lax
from jax.experimental import pallas as pl
from jax.experimental.pallas import tpu as pltpu
from jax.sharding import PartitionSpec as P

VMEM = pl.BlockSpec(memory_space=pltpu.VMEM)
ANY = pl.BlockSpec(memory_space=pl.ANY)
MOST = 63 * 1024 * 1024
LANES = 128
HALF_ROOT = math.sqrt(0.75)
LIMIT = 20 * 1024 * 1024


def lanes_waves():
    angles = 2.0 * np.pi / LANES * (np.outer(np.arange(LANES), np.arange(LANES)) % LANES)
    return jnp.asarray(np.stack([np.cos(angles), np.sin(angles)]), jnp.bfloat16)


def fill_tables(waves_ref, table_ref, back_ref):
    cos, sin = waves_ref[0], waves_ref[1]
    for row, parts in enumerate([(cos, -sin, cos, -sin), (sin, cos, -sin, -cos)]):
        for col, part in enumerate(parts):
            table_ref[row * LANES : (row + 1) * LANES, col * LANES : (col + 1) * LANES] = part
    for row, parts in enumerate([(cos, sin), (sin, -cos), (cos, -sin), (sin, cos)]):
        for col, part in enumerate(parts):
            back_ref[row * LANES : (row + 1) * LANES, col * LANES : (col + 1) * LANES] = part


def twist_rows(half):
    angles = np.pi / (half * LANES) * np.outer(np.arange(half + 1), np.arange(LANES))
    return jnp.asarray(np.concatenate([np.cos(angles), -np.sin(angles)]), jnp.float32)


def window_width(share, count):
    return -(-(share + 2 * count) // LANES) * LANES


def fill_shares(shares_ref, share, wide):
    length, columns = shares_ref.shape
    line = lax.broadcasted_iota(jnp.int32, (length, wide), 0)
    lane = lax.broadcasted_iota(jnp.int32, (length, wide), 1)
    for part in range(columns // wide):
        chosen = jnp.logical_and(lane < share, line == lane + part * share)
        shares_ref[:, part * wide : (part + 1) * wide] = chosen.astype(jnp.bfloat16)


def times(pair, k, size, direction):
    re, im = pair
    cos, sin = math.cos(2 * math.pi * k / size), direction * math.sin(2 * math.pi * k / size)
    return re * cos - im * sin, re * sin + im * cos


def forward_half(values):
    if len(values) == 1:
        return [(values[0], None), (values[0], None)]
    if len(values) == 3:
        both, gap = values[1] + values[2], values[1] - values[2]
        return [
            (values[0] + both, None),
            (values[0] + 0.5 * gap, -HALF_ROOT * both),
            (values[0] - 0.5 * both, -HALF_ROOT * gap),
            (values[0] - gap, None),
        ]
    even, odd = forward_half(values[0::2]), forward_half(values[1::2])
    half = len(values)
    quarter = half // 2
    out = [None] * (half + 1)
    out[0] = (even[0][0] + odd[0][0], None)
    out[half] = (even[0][0] - odd[0][0], None)
    out[quarter] = (even[quarter][0], -odd[quarter][0])
    for k in range(1, quarter):
        re, im = times(odd[k], k, 2 * half, -1.0)
        out[k] = (even[k][0] + re, even[k][1] + im)
        out[half - k] = (even[k][0] - re, im - even[k][1])
    return out


def inverse_half(bins):
    half = len(bins) - 1
    if half == 1:
        return [bins[0][0] + bins[1][0]]
    if half == 3:
        (zero, _), (re, im), (re_two, im_two), (three, _) = bins
        both, gap = zero + three, zero - three
        return [
            both + 2.0 * (re + re_two),
            gap + (re - re_two) - 2.0 * HALF_ROOT * (im + im_two),
            both - (re + re_two) - 2.0 * HALF_ROOT * (im - im_two),
        ]
    quarter = half // 2
    even = [(bins[0][0] + bins[half][0], None)]
    odd = [(bins[0][0] - bins[half][0], None)]
    for k in range(1, quarter):
        (a, b), (c, d) = bins[k], bins[half - k]
        even.append((a + c, b - d))
        odd.append(times((a - c, b + d), k, 2 * half, 1.0))
    even.append((2.0 * bins[quarter][0], None))
    odd.append((-2.0 * bins[quarter][1], None))
    out = [None] * half
    out[0::2] = inverse_half(even)
    out[1::2] = inverse_half(odd)
    return out


def spectra_kernel(spectra_ref, out_ref, arriving, leaving, sems_in, sems_out):
    orders, parts, residues = spectra_ref.shape[:3]
    count, slabs, each, length = out_ref.shape
    steps, groups = length // LANES, arriving.shape[1]
    fetches, stores = [], []
    for i in range(slabs):
        order, part, residue = i // (parts * residues), i // residues % parts, i % residues
        for group in range(groups):
            source = spectra_ref.at[order, part, residue, :, pl.ds(group * LANES, LANES)]
            fetches.append(pltpu.make_async_copy(source, arriving.at[i, group], sems_in.at[i, group]))
        stores.append(pltpu.make_async_copy(leaving.at[i], out_ref.at[:, i], sems_out.at[i]))
    for fetch in fetches:
        fetch.start()
    some = count // groups
    for i, store in enumerate(stores):
        runs = []
        for group in range(groups):
            fetches[i * groups + group].wait()
            runs.append(jnp.concatenate([arriving[i, group, pl.ds(start, LANES, stride=steps), :] for start in range(steps)], axis=0))
        leaving[i] = jnp.concatenate(runs, axis=1).astype(jnp.bfloat16).T.reshape(count, each, length)
        store.start()
    for store in stores:
        store.wait()


def send_spectra(spectra, count):
    orders, parts, residues, length, channels = spectra.shape
    each = channels // count
    slabs = orders * parts * residues
    return pl.pallas_call(
        spectra_kernel,
        in_specs=[ANY],
        out_specs=ANY,
        out_shape=jax.ShapeDtypeStruct((count, slabs, each, length), jnp.bfloat16),
        scratch_shapes=[
            pltpu.VMEM((slabs, channels // LANES, length, LANES), jnp.float32),
            pltpu.VMEM((slabs, count, each, length), jnp.bfloat16),
            pltpu.SemaphoreType.DMA((slabs, channels // LANES)),
            pltpu.SemaphoreType.DMA((slabs,)),
        ],
        compiler_params=pltpu.CompilerParams(vmem_limit_bytes=MOST),
    )(spectra)


def tap_columns(taps_ref, skip_ref, gathered):
    branches = taps_ref.shape[0]
    for branch in range(branches):
        gathered[branch * 3 : branch * 3 + 3] = taps_ref[branch]
    gathered[9:11] = skip_ref[...]
    return gathered[...].T


def filter_lines(now, last, scale, lane):
    total = scale[0] * now
    rolls = []
    for back in (1, 2):
        rolled = pltpu.roll(now, back, 1)
        total = total + scale[back] * jnp.where(lane < back, last[back - 1], rolled)
        rolls.append(rolled)
    return total, rolls


def project_kernel(tokens_ref, weight_ref, taps_ref, skip_ref, *refs):
    mine_ref, other_ref, edge_ref = refs[:3]
    outs, (held, gathered, windows) = refs[3:-3], refs[-3:]
    count, pieces, each, length = held.shape
    across, channels, wide = windows.shape
    share = pieces * length // across
    branch = pl.program_id(0)
    me = lax.axis_index("seq")
    rows = jnp.dot(tokens_ref[...], weight_ref[0], preferred_element_type=jnp.float32)
    turned = [rows[piece * length : (piece + 1) * length].T for piece in range(pieces)]

    @pl.when(branch < 2)
    def _():
        for piece in range(pieces):
            held[:, piece] = turned[piece].reshape(count, each, length).astype(jnp.bfloat16)
        for shift in range(count // 2):
            to = lax.rem(me + 2 * shift, count)
            mine_ref[shift, 0] = held[to]
            other_ref[shift, 0] = held[jnp.bitwise_xor(to, 1)]

    @pl.when(branch == 2)
    def _():
        columns = tap_columns(taps_ref, skip_ref, gathered)
        scale = [jnp.broadcast_to(columns[:, 6 + i : 7 + i], (channels, length)) for i in range(3)]
        lane = lax.broadcasted_iota(jnp.int32, (channels, length), 1)
        last = [jnp.zeros((channels, length), jnp.float32)] * 2
        windows[...] = jnp.zeros_like(windows)
        for piece in range(pieces):
            now = turned[piece].astype(jnp.bfloat16).astype(jnp.float32)
            total, last = filter_lines(now, last, scale, lane)
            for part in range(length // share):
                window = total[:, part * share : (part + 1) * share]
                windows[piece * (length // share) + part, :, :share] = window.astype(jnp.bfloat16)
        for flip, out in enumerate(outs):
            out[...] = windows[jnp.bitwise_xor(lax.axis_index("tp"), flip)]
        edge = jnp.where(lane < 1, scale[1] * last[0], 0.0) + jnp.where(lane < 2, scale[2] * last[1], 0.0)
        edge = edge[:, :LANES] * (me < count - 1).astype(jnp.float32)
        if wide > LANES:
            edge = jnp.concatenate([edge, jnp.zeros((channels, wide - LANES), jnp.float32)], axis=1)
        total = jnp.zeros((each, wide), jnp.float32)
        for block in range(count):
            total = total + pltpu.roll(edge[block * each : (block + 1) * each], share + 2 * block, 1)
        edge_ref[...] = total.astype(jnp.bfloat16)


def project(tokens, weights, taps, skip, count, across, length):
    rows, depth = tokens.shape
    branches, _, channels = weights.shape
    each, pieces = channels // count, rows // length
    wide = window_width(rows // across, count)
    half = (count // 2, 1, pieces, each, length)
    return pl.pallas_call(
        project_kernel,
        grid=(branches,),
        in_specs=[
            pl.BlockSpec((rows, depth), lambda b: (0, 0)),
            pl.BlockSpec((1, depth, channels), lambda b: (b, 0, 0)),
            pl.BlockSpec(taps.shape, lambda b: (0, 0, 0)),
            pl.BlockSpec(skip.shape, lambda b: (0, 0)),
        ],
        out_specs=[
            pl.BlockSpec(half, lambda b: (0, jnp.minimum(b, 1), 0, 0, 0)),
            pl.BlockSpec(half, lambda b: (0, jnp.minimum(b, 1), 0, 0, 0)),
            pl.BlockSpec((each, wide), lambda b: (0, 0)),
        ]
        + [pl.BlockSpec((channels, wide), lambda b: (0, 0))] * across,
        out_shape=[
            jax.ShapeDtypeStruct((count // 2, 2) + half[2:], jnp.bfloat16),
            jax.ShapeDtypeStruct((count // 2, 2) + half[2:], jnp.bfloat16),
            jax.ShapeDtypeStruct((each, wide), jnp.bfloat16),
        ]
        + [jax.ShapeDtypeStruct((channels, wide), jnp.bfloat16)] * across,
        scratch_shapes=[
            pltpu.VMEM((count, pieces, each, length), jnp.bfloat16),
            pltpu.VMEM((16, channels), jnp.float32),
            pltpu.VMEM((across, channels, wide), jnp.bfloat16),
        ],
        compiler_params=pltpu.CompilerParams(vmem_limit_bytes=LIMIT),
    )(tokens, weights, taps, skip)


def pack_kernel(weight_ref, *refs):
    windows, outs = refs[: len(refs) // 2], refs[len(refs) // 2 :]
    for window, out in zip(windows, outs):
        wide = window.shape[1]
        out[:, :wide] = window[...]
        out[:, wide:] = weight_ref[...]


def pack(windows, weight):
    channels, wide = windows[0].shape
    shape = jax.ShapeDtypeStruct((channels, wide + weight.shape[1]), jnp.bfloat16)
    return pl.pallas_call(
        pack_kernel,
        in_specs=[VMEM] * (1 + len(windows)),
        out_specs=[VMEM] * len(windows),
        out_shape=[shape] * len(windows),
        compiler_params=pltpu.CompilerParams(vmem_limit_bytes=LIMIT),
    )(weight, *windows)


def relay_kernel(mine_ref, came_ref, *outs):
    for shift, out in enumerate(outs, 1):
        out[0] = mine_ref[shift]
        out[1] = came_ref[shift]


def relay(mine, came):
    shape = (2,) + mine.shape[1:]
    return pl.pallas_call(
        relay_kernel,
        in_specs=[VMEM] * 2,
        out_specs=[VMEM] * (mine.shape[0] - 1),
        out_shape=[jax.ShapeDtypeStruct(shape, jnp.bfloat16)] * (mine.shape[0] - 1),
        compiler_params=pltpu.CompilerParams(vmem_limit_bytes=LIMIT),
    )(mine, came)


def forward_tile(values, rows, lines, twist_ref, each):
    bins = forward_half(values)
    for k, (re, im) in enumerate(bins):
        cos, sin = twist_ref[k : k + 1], twist_ref[len(bins) + k : len(bins) + k + 1]
        pair = (re * cos, re * sin) if im is None else (re * cos - im * sin, re * sin + im * cos)
        at = slice(k * each + rows.start, k * each + rows.stop)
        for part in range(2):
            lines[at, part * LANES : (part + 1) * LANES] = pair[part].astype(jnp.bfloat16)


def respond(spectrum, start, order, spectra_ref, answers, each, blocks, half):
    residues = spectra_ref.shape[1] // 4
    for k in range(start // each, (start + spectrum.shape[0]) // each):
        at = k * each - start
        for mirror in range(2 if 0 < k < half else 1):
            col = 2 * mirror * LANES
            re, im = spectrum[at : at + each, col : col + LANES], spectrum[at : at + each, col + LANES : col + 2 * LANES]
            bin_at = 2 * half - k if mirror else k
            block, cols = bin_at % blocks, slice(bin_at // blocks * LANES, (bin_at // blocks + 1) * LANES)
            first = order * 2 * residues + block % residues
            gain_re = spectra_ref[block // residues, first, :, cols].astype(jnp.float32)
            gain_im = spectra_ref[block // residues, first + residues, :, cols].astype(jnp.float32)
            if mirror:
                gain_re, gain_im = pltpu.roll(gain_re, 1, 1), pltpu.roll(gain_im, 1, 1)
            rows = slice(k * each, (k + 1) * each)
            answers[rows, col : col + LANES] = (re * gain_re - im * gain_im).astype(jnp.bfloat16)
            answers[rows, col + LANES : col + 2 * LANES] = (-(re * gain_im) - im * gain_re).astype(jnp.bfloat16)


def inverse_tile(wave, rows, twist_ref, half, each):
    bins = []
    for k in range(half + 1):
        cos, sin = twist_ref[k : k + 1], twist_ref[half + 1 + k : half + 2 + k]
        at = slice(k * each + rows.start, k * each + rows.stop)
        re, im = wave[at, :LANES], wave[at, LANES:]
        if k in (0, half):
            bins.append((2.0 * (re * cos + im * sin), None))
        else:
            bins.append((re * cos + im * sin, im * cos - re * sin))
    return [value * (0.25 / (half * LANES)) for value in inverse_half(bins)]


def row_steps(total, step):
    return [slice(start, min(start + step, total)) for start in range(0, total, step)]


def flipped(array, flip, size):
    return lax.ppermute(array, "tp", [(i, i ^ flip) for i in range(size)])


def convolve_kernel(*refs):
    mine_in, came_in, spectra_in, twist_ref, waves_ref, taps_ref, skip_ref, edge_ref = refs[:8]
    shifted, refs = refs[8:-13], refs[-13:]
    out_ref, held, spectra_ref, table_ref, back_ref, shares_ref, filtered, lines, answers, wave = refs[:10]
    gathered, columns, sems = refs[10:]
    branches, positions, each, length = filtered.shape
    blocks = 2 * positions
    runs = length // LANES
    count = held.shape[0]
    pieces = positions // count
    slabs = spectra_ref.shape[1]
    me = lax.axis_index("seq")
    other = jnp.bitwise_xor(me, 1)

    held[me] = mine_in[0]
    held[other] = came_in[0]
    for shift, ref in enumerate(shifted, 1):
        for i, one in enumerate((me, other)):
            held[lax.rem(one + count - 2 * shift, count)] = ref[i]
    halves = [slice(0, slabs // 2), slice(slabs // 2, slabs)]
    spectra = [
        pltpu.make_async_copy(spectra_in.at[:, half], spectra_ref.at[:, half], sems.at[1 + i])
        for i, half in enumerate(halves)
    ]
    for copy in spectra:
        copy.start()
    columns[...] = tap_columns(taps_ref, skip_ref, gathered)
    mine = columns[pl.ds(pl.multiple_of(me * each, each), each), :]
    lane = lax.broadcasted_iota(jnp.int32, (each, length), 1)
    fill_tables(waves_ref, table_ref, back_ref)
    wide = out_ref.shape[3]
    fill_shares(shares_ref, pieces * length // out_ref.shape[1], wide)
    for branch in range(branches):
        last = [jnp.zeros((each, length), jnp.float32)] * 2
        scale = [jnp.broadcast_to(mine[:, branch * 3 + i : branch * 3 + i + 1], (each, length)) for i in range(3)]
        for p in range(positions):
            now = held[p // pieces, branch, p % pieces].astype(jnp.float32)
            filtered[branch, p], last = filter_lines(now, last, scale, lane)
    skips = [jnp.broadcast_to(mine[:, 9 + order : 10 + order], (each, LANES)) for order in range(2)]

    half = runs * positions
    steps = row_steps((half + 1) * each, max(1, 416 // each) * each)
    for k in (0, half):
        answers[k * each : (k + 1) * each, 2 * LANES :] = jnp.zeros((each, 2 * LANES), jnp.bfloat16)

    def through(order):
        spectra[order].wait()
        for rows in steps:
            spectrum = jnp.dot(lines[rows], table_ref[...], preferred_element_type=jnp.float32)
            respond(spectrum, rows.start, order, spectra_ref, answers, each, blocks, half)
        for rows in steps:
            wave[rows] = jnp.dot(answers[rows], back_ref[...], preferred_element_type=jnp.float32)

    chunk = min(16, each)
    tiles = [slice(row, row + chunk) for row in range(0, each, chunk)]
    places = [(p, slice(run * LANES, (run + 1) * LANES)) for p in range(positions) for run in range(runs)]
    for rows in tiles:
        forward_tile([filtered[0, p, rows, cols] for p, cols in places], rows, lines, twist_ref, each)
    through(0)
    for rows in tiles:
        values = inverse_tile(wave, rows, twist_ref, len(places), each)
        for i, (p, cols) in enumerate(places):
            values[i] = filtered[1, p, rows, cols] * (values[i] + skips[0][rows] * filtered[0, p, rows, cols])
            filtered[0, p, rows, cols] = values[i]
        forward_tile(values, rows, lines, twist_ref, each)
    through(1)
    for rows in tiles:
        values = inverse_tile(wave, rows, twist_ref, len(places), each)
        for value, (p, cols) in zip(values, places):
            filtered[0, p, rows, cols] = value + skips[1][rows] * filtered[0, p, rows, cols]
    parts = shares_ref.shape[1] // wide
    following = lax.rem(me + 1, count)
    leaving = out_ref
    for some_p in (range(positions // 2), range(positions // 2, positions)):
        flat = filtered[0, some_p.start : some_p.stop].reshape(len(some_p) * each, length).astype(jnp.bfloat16)
        spread_out = jnp.dot(flat, shares_ref[...], preferred_element_type=jnp.float32)
        for at, p in enumerate(some_p):
            for part in range(parts):
                block = spread_out[at * each : (at + 1) * each, part * wide : (part + 1) * wide]
                leaving[p // pieces, p % pieces * parts + part] = block.astype(jnp.bfloat16)
        half_count = slice(some_p.start // pieces, some_p.stop // pieces)
        here = jnp.logical_and(following >= half_count.start, following < half_count.stop)

        @pl.when(here)
        def _():
            leaving[following, 0] = leaving[following, 0] + edge_ref[...]


def convolve(mine, came, shifted, spectra, taps, skip, edge, across):
    count, slabs, each, length = spectra.shape
    branches, pieces = mine.shape[1:3]
    positions = count * pieces
    blocks = 2 * positions
    channels = taps.shape[2]
    half = length // LANES * positions
    twist, waves = twist_rows(half), lanes_waves()
    share = pieces * length // across
    wide = window_width(share, count)
    return pl.pallas_call(
        convolve_kernel,
        in_specs=[VMEM] * 2 + [ANY] + [VMEM] * 5 + [VMEM] * len(shifted),
        out_specs=VMEM,
        out_shape=jax.ShapeDtypeStruct((count, across, each, wide), jnp.bfloat16),
        scratch_shapes=[
            pltpu.VMEM((count, branches, pieces, each, length), jnp.bfloat16),
            pltpu.VMEM(spectra.shape, spectra.dtype),
            pltpu.VMEM((2 * LANES, 4 * LANES), jnp.bfloat16),
            pltpu.VMEM((4 * LANES, 2 * LANES), jnp.bfloat16),
            pltpu.VMEM((length, length // share * wide), jnp.bfloat16),
            pltpu.VMEM((branches, positions, each, length), jnp.float32),
            pltpu.VMEM(((half + 1) * each, 2 * LANES), jnp.bfloat16),
            pltpu.VMEM(((half + 1) * each, 4 * LANES), jnp.bfloat16),
            pltpu.VMEM(((half + 1) * each, 2 * LANES), jnp.float32),
            pltpu.VMEM((16, channels), jnp.float32),
            pltpu.VMEM((channels, 16), jnp.float32),
            pltpu.SemaphoreType.DMA((4,)),
        ],
        compiler_params=pltpu.CompilerParams(vmem_limit_bytes=52 * 1024 * 1024),
    )(mine, came, spectra, twist, waves, taps, skip, edge, *shifted)


def finish_kernel(share, carried_ref, own_ref, weight_ref, *refs):
    came, out_ref = refs[:-1], refs[-1]
    count, across, each, wide = carried_ref.shape
    me = lax.axis_index("tp")
    before = lax.rem(lax.axis_index("seq") + count - 1, count)
    first = (me == 0).astype(jnp.float32)
    lane = lax.broadcasted_iota(jnp.int32, (each, wide), 1)
    pairs = [(own_ref[...], weight_ref[...])] + [(ref[:, :wide], ref[:, wide:]) for ref in came]
    total = jnp.zeros((wide, out_ref.shape[1]), jnp.float32)
    for flip, (gate, weight) in enumerate(pairs):
        source = jnp.bitwise_xor(me, flip)
        edge = carried_ref[before, source].astype(jnp.float32) * first
        edges = [
            jnp.where(lane < 2, pltpu.roll(edge, wide - share - 2 * block, 1), 0.0) for block in range(count)
        ]
        gate = gate.astype(jnp.float32) + jnp.concatenate(edges, axis=0)
        part = carried_ref[:, source].astype(jnp.float32).reshape(count * each, wide)
        total = total + lax.dot_general(
            (part * gate).astype(jnp.bfloat16), weight, (((0,), (0,)), ((), ())), preferred_element_type=jnp.float32
        )
    out_ref[...] = total[:share].astype(jnp.bfloat16)


def finish(carried, own, weight, came, share):
    return pl.pallas_call(
        functools.partial(finish_kernel, share),
        in_specs=[VMEM] * (3 + len(came)),
        out_specs=VMEM,
        out_shape=jax.ShapeDtypeStruct((share, weight.shape[1]), jnp.bfloat16),
        compiler_params=pltpu.CompilerParams(vmem_limit_bytes=LIMIT),
    )(carried, own, weight, *came)


def spread(array, axes):
    return lax.all_to_all(array, axes, split_axis=0, concat_axis=0, tiled=True)


def local(tokens, w_in, short_taps, skip_bias, filter_spectra, w_out):
    count, across = lax.axis_size("seq"), lax.axis_size("tp")
    length = filter_spectra.shape[3]
    spectra = spread(send_spectra(filter_spectra, count), "seq")
    gathered = lax.all_gather(tokens, "tp", axis=0, tiled=True)
    mine, other, edge, own, *windows = project(gathered, w_in, short_taps, skip_bias, count, across, length)
    came = lax.ppermute(other, "seq", [(i, i ^ 1) for i in range(count)])
    came, *packed = lax.optimization_barrier((came, *pack(windows, w_out)))
    onward = relay(mine, came)
    shifted = [
        lax.ppermute(array, "seq", [(i, (i + 2 * shift) % count) for i in range(count)])
        for shift, array in enumerate(onward, 1)
    ]
    packed = [flipped(array, flip, across) for flip, array in enumerate(packed, 1)]
    carried = convolve(mine, came, shifted, spectra, short_taps, skip_bias, edge, across)
    shape = carried.shape
    carried = spread(carried.reshape((count * across,) + shape[2:]), ("seq", "tp"))
    return finish(carried.reshape(shape), own, w_out, packed, tokens.shape[0])


def solution(mesh):
    in_specs = (
        P(("seq", "tp"), None),
        P(None, None, "tp"),
        P(None, None, "tp"),
        P(None, "tp"),
        P(None, None, "seq", None, "tp"),
        P("tp", None),
    )
    out_specs = P(("seq", "tp"), None)
    return jax.shard_map(local, mesh=mesh, in_specs=in_specs, out_specs=out_specs, check_vma=False)
```
